256 devices in a mesh: seq: 64 (over x, y, z_hi, core), head: 4 (over z_lo).
Axes of the slice: x: 4, y: 4, z: 8 (z_hi: 2, z_lo: 4; z = z_hi * 4 + z_lo), core: 2. Of those that a mesh axis runs over, the one named last changes fastest.
Arguments:
- queries: bfloat16 [12288, 64, 128], P('seq', 'head'), may hold values from -160 to 160
- keys: bfloat16 [12288, 8, 128], P(('seq', 'head')), may hold values from -8 to 8
- values: bfloat16 [12288, 8, 128], P(('seq', 'head')), may hold values from -6 to 6
- doc_ids: int32 [12288], P('seq'), may hold values from 0 to 15, never falling along the last dimension, each value on 1 to 6336 neighbouring positions
Outputs:
- attended: bfloat16 [12288, 64, 128], P('seq', 'head')
The draws below stay inside these ranges and needn't reach their ends.
Inputs may be any that keep to these rules, and one draw needn't show every extreme that they name: `doc_ids`: documents are runs of consecutive positions; the longest holds exactly 6336 positions.
All inputs are finite; a program needn't handle non-finite values.
Results may differ from the reference program's by a relative error of at most 0.0059.
Values may be sent and summed in bfloat16 or wider, within the bound.
A program may use at most 64 MiB of HBM per device.

```python
import math
import jax
import jax.numpy as jnp
import numpy as np
from jax import lax

HEADS = 64
KV_HEADS = 8
HEAD_DIM = 128
TOKENS = 12288
DOC_MOST = 6336
DOCS = 16


def paired(key):
    query_key = jax.random.fold_in(key, 11)
    key_key = jax.random.fold_in(key, 12)
    qdraw = jnp.clip(jax.random.normal(query_key, (TOKENS, HEADS, HEAD_DIM), jnp.float32), -6.0, 6.0)
    kdraw = jnp.clip(jax.random.normal(key_key, (TOKENS, KV_HEADS, HEAD_DIM), jnp.float32), -6.0, 6.0)
    return (qdraw.astype(jnp.bfloat16), kdraw.astype(jnp.bfloat16))


def draw_queries(key, part):
    return paired(key)[0]


def draw_keys(key, part):
    return paired(key)[1]


def block_scale(key, extent, shards, low, largest):
    def one(dim, shards_of):
        heights = jax.random.uniform(jax.random.fold_in(jax.random.fold_in(key, 6), dim), (shards_of,), jnp.float32, low / len(shards), largest / len(shards))
        return jnp.repeat(jnp.exp(heights), extent[dim] // shards_of).reshape((-1,) + (1,) * (len(extent) - dim - 1))

    level = one(*shards[0])
    for cut in shards[1:]:
        level = level * one(*cut)
    return level


def profile(amount, total, most, skew):
    weights = [(1 << 20) // math.isqrt(rank ** skew) + 1 for rank in range(2, amount + 1)]
    spare, counts = total - most - (amount - 1), [1] * (amount - 1)
    while spare > 0:
        free = [i for i in range(amount - 1) if counts[i] < most]
        mass, left = sum([weights[i] for i in free]), spare
        for i in free:
            extra = min(most - counts[i], max(1, left * weights[i] // mass), spare)
            counts[i] = counts[i] + extra
            spare = spare - extra
    return np.array([most] + counts)


def uneven_parts(own_key, number_of, total, limit, lean):
    if number_of == 2:
        one = jax.random.randint(own_key, (), max(1, total - limit), min(limit, total - 1) + 1)
        return jnp.stack([one, total - one])
    lengths = jnp.asarray(profile(number_of, total, limit, lean), jnp.int32)
    twos = (number_of - 1) // 2
    donor, taker = lengths[1:1 + 2 * twos:2], lengths[2:2 + 2 * twos:2]
    margin = jnp.minimum(donor - 1, limit - taker)
    moved = jax.random.randint(jax.random.fold_in(own_key, 1), (twos,), 0, 1 << 20) % (margin + 1)
    lengths = lengths.at[1:1 + 2 * twos:2].set(donor - moved).at[2:2 + 2 * twos:2].set(taker + moved)
    return lengths[jax.random.permutation(jax.random.fold_in(own_key, 2), number_of)]


def scatter_about(key, dims, width, bound, cuts=(), kind=jnp.bfloat16):
    drawn = jax.random.normal(key, dims, jnp.float32) * width
    if len(cuts) > 0:
        drawn = block_scale(key, dims, cuts, -0.22, 0.18) * drawn
    return jnp.clip(drawn, min=-bound, max=bound).astype(kind)


def setup_inputs(seed: int = 0) -> dict:
    streams_of = jax.random.split(jax.random.key(seed), 5)
    return {
        "queries": draw_queries(jax.random.fold_in(streams_of[4], 71), 0),
        "keys": draw_keys(jax.random.fold_in(streams_of[4], 71), 0),
        "values": scatter_about(streams_of[2], (TOKENS, KV_HEADS, HEAD_DIM), 1.0, 6.0, ((0, 256),)),
        "doc_ids": jnp.searchsorted(jnp.cumsum(uneven_parts(streams_of[3], DOCS, TOKENS, DOC_MOST, 2)), jnp.arange(TOKENS), side="right").astype(jnp.int32),
    }


def reference(queries, keys, values, doc_ids):
    group = HEADS // KV_HEADS
    block = math.gcd(TOKENS, 256)
    span = min(DOC_MOST + block, TOKENS)
    scale = HEAD_DIM ** -0.5
    positions = jnp.arange(TOKENS, dtype=jnp.int32)

    def one_block(index):
        start = (index * block).astype(jnp.int32)
        kstart = jnp.clip(start + block - span, 0, TOKENS - span).astype(jnp.int32)
        qrows = lax.dynamic_slice_in_dim(queries, start, block, 0).astype(jnp.float32)
        qrows = qrows.reshape(block, KV_HEADS, group, HEAD_DIM)
        krows = lax.dynamic_slice_in_dim(keys, kstart, span, 0).astype(jnp.float32)
        vrows = lax.dynamic_slice_in_dim(values, kstart, span, 0).astype(jnp.float32)
        qpos = lax.dynamic_slice_in_dim(positions, start, block, 0)
        kpos = lax.dynamic_slice_in_dim(positions, kstart, span, 0)
        qdoc = lax.dynamic_slice_in_dim(doc_ids, start, block, 0)
        kdoc = lax.dynamic_slice_in_dim(doc_ids, kstart, span, 0)
        allowed = (kpos[None, :] <= qpos[:, None]) & (kdoc[None, :] == qdoc[:, None])
        scores = jnp.einsum("qkgd,pkd->kgqp", qrows, krows) * scale
        scores = jnp.where(allowed[None, None], scores, -1e30)
        top = jnp.max(scores, axis=-1, keepdims=True)
        weights = jnp.where(allowed[None, None], jnp.exp(scores - top), 0.0)
        total = jnp.sum(weights, axis=-1)
        rounded = weights.astype(jnp.bfloat16).astype(jnp.float32)
        mixed = jnp.einsum("kgqp,pkd->qkgd", rounded, vrows)
        mixed = mixed / jnp.transpose(total, (2, 0, 1))[..., None]
        return mixed.reshape(block, HEADS, HEAD_DIM).astype(jnp.bfloat16)

    pieces = lax.map(one_block, jnp.arange(TOKENS // block, dtype=jnp.int32))
    return pieces.reshape(TOKENS, HEADS, HEAD_DIM)
```

```python
import functools
import math

import jax
import jax.numpy as jnp
from jax import lax
from jax.experimental import pallas as pl
from jax.experimental.pallas import tpu as pltpu
from jax.sharding import PartitionSpec as P

MESH = pl.DeviceIdType.MESH

ROWS = 192
PIECE = 48
GROUP = 8
D = 128
HALF = 2 * ROWS
CHUNK = HALF + 16
KEYS = 2 * HALF
M = 2 * ROWS * GROUP
MC = ROWS * GROUP
SUB = 256
FAR = 2.0**20
SCALE = (1.0 / math.sqrt(D)) * math.log2(math.e)

PLAN = (
    ((1, 0, 1, 1, 1), (1, 1, 0, 0, 1), (1, 3, 0, 1, 0), (2, 0, 0, 0, 0),
     (1, 2, 0, 0, 0), (2, 1, 0, 0, 0), (2, 3, 0, 0, 0), (2, 2, 0, 0, 0)),
    ((0, 0, 0, 1, 0), (1, 1, 1, 1, 1), (1, 0, 0, 0, 0), (1, 2, 0, 0, 0),
     (2, 1, 0, 0, 1), (1, 3, 0, 0, 0), (2, 2, 0, 0, 1), (2, 3, 0, 0, 0)),
    ((0, 1, 0, 1, 0), (1, 2, 1, 1, 1), (0, 0, 0, 0, 0), (1, 1, 0, 0, 0),
     (1, 3, 0, 0, 0), (2, 2, 0, 0, 1), (1, 0, 0, 0, 0), (2, 3, 0, 0, 1)),
    ((0, 2, 0, 0, 0), (0, 0, 0, 0, 0), (1, 3, 1, 1, 1), (0, 1, 0, 0, 0),
     (1, 2, 0, 1, 0), (1, 0, 0, 0, 1), (2, 3, 0, 1, 1), (1, 1, 0, 0, 0)),
)
STEPS = len(PLAN[0])


def packed(field):
    return [sum(step[field] << (2 * k) for k, step in enumerate(lane)) for lane in PLAN]


BACK, LANE, GOX, GOP, GOM = (packed(f) for f in range(5))


def pick(table, y, k):
    value = jnp.int32(table[3])
    for lane in range(3):
        value = jnp.where(y == lane, jnp.int32(table[lane]), value)
    return lax.shift_right_logical(value, 2 * k) & 3


def kernel(q_ref, k_ref, v_ref, id_ref, o_ref,
           wide, snd, kv, qst, qaug, feat, ones, top, acc, obuf,
           zsend, zrecv, lsem, qsend, qrecv, osend, orecv, ssem, rsem, qtr):
    s = lax.axis_index("seq")
    g = lax.axis_index("head")
    x, y, zh, c = s // 16, (s // 4) % 4, (s // 2) % 2, s % 2
    col = s // 4
    low = s % 4

    def at(xx, yy):
        return ((xx * 4 + yy) * 4 + low, g)

    def inside(dz, dc, dg):
        return (col * 4 + ((zh + dz) % 2) * 2 + (c + dc) % 2, (g + dg) % 4)

    sibling = inside(0, 1, 0)
    east = at((x + 1) % 4, y)
    plus = at(x, (y + 1) % 4)
    minus = at(x, (y + 3) % 4)
    others = [(dz, dc, dg) for dz in (0, 1) for dg in (0, 1, 3, 2) for dc in (0, 1) if dz or dc or dg]

    barrier = pltpu.get_barrier_semaphore()
    peers = [inside(*o) for o in others] + [east, at((x + 3) % 4, y), plus, minus]
    for peer in peers:
        pl.semaphore_signal(barrier, inc=1, device_id=peer, device_id_type=MESH)

    for which, ref in enumerate((k_ref, v_ref)):
        wide[...] = ref[...].astype(jnp.float32)
        for h in range(8):
            snd[h, which] = wide[pl.ds(h, PIECE, stride=8), :].astype(jnp.bfloat16)

    ids = id_ref[...].astype(jnp.float32)
    first = ids[:, :D]
    second = jnp.concatenate([ids[:, D:], jnp.zeros((1, 2 * D - ROWS), jnp.float32)], axis=1)
    tile = jnp.concatenate([first, second, jnp.zeros((14, D), jnp.float32)], axis=0)
    block = 2 * zh + c
    kv[col, block, HALF:, :] = tile.astype(jnp.bfloat16)

    pl.semaphore_wait(barrier, len(peers))

    spot = pl.multiple_of(PIECE * g, 16)
    for o in others:
        dz, dc, dg = o
        head = 2 * ((g + dg) % 4) + (c + dc) % 2
        for which in range(2):
            pltpu.make_async_remote_copy(
                src_ref=snd.at[head, which],
                dst_ref=kv.at[col, block, pl.ds(spot + which * ROWS, PIECE)],
                send_sem=zsend.at[dz], recv_sem=zrecv.at[block],
                device_id=inside(*o), device_id_type=MESH).start()
        if dg == 0:
            pltpu.make_async_remote_copy(
                src_ref=kv.at[col, block, pl.ds(HALF, 16)], dst_ref=kv.at[col, block, pl.ds(HALF, 16)],
                send_sem=zsend.at[dz], recv_sem=zrecv.at[block],
                device_id=inside(*o), device_id_type=MESH).start()
    for which in range(2):
        pltpu.make_async_copy(snd.at[2 * g + c, which], kv.at[col, block, pl.ds(spot + which * ROWS, PIECE)],
                              lsem.at[0]).start()

    def wait_rows(sem, n):
        pltpu.make_async_copy(feat.at[pl.ds(0, n)], feat.at[pl.ds(0, n)], sem).wait()

    turned = jnp.transpose(tile[:8])
    lanes = lax.broadcasted_iota(jnp.int32, (D, D), 1).astype(jnp.float32)
    for part, size in ((0, D), (1, ROWS - D)):
        hot = jnp.where(turned[:size, part:part + 1] == lanes[:size], 1.0, 0.0)
        hot = jnp.broadcast_to(hot[:, None, :], (size, GROUP, D)).reshape(size * GROUP, D)
        for which in range(2):
            qst[which, pl.ds(part * D * GROUP, size * GROUP), D:] = hot.astype(jnp.bfloat16)

    def split(t, carry):
        rows = q_ref[pl.ds(t * 16 * 16, 256), :].astype(jnp.float32).reshape(16, 16, D)
        for which in range(2):
            qst[which, pl.ds(t * 128, 128), :D] = (
                rows[:, 8 * which:8 * which + 8, :].reshape(128, D).astype(jnp.bfloat16))
        return carry

    lax.fori_loop(0, ROWS // 16, split, 0)
    base = pl.multiple_of(c * MC, MC)
    qcopy = pltpu.make_async_remote_copy(
        src_ref=qst.at[1 - c], dst_ref=qaug.at[pl.ds(base, MC)],
        send_sem=qsend, recv_sem=qrecv, device_id=sibling, device_id_type=MESH)
    qcopy.start()
    qlocal = pltpu.make_async_copy(qst.at[c], qaug.at[pl.ds(base, MC)], lsem.at[1])
    qlocal.start()
    ones[...] = jnp.ones_like(ones)

    def order(t):
        return 2 * ((zh + t // 2) % 2) + (c + t) % 2

    def hands(step, who, b, gox, gop, gom):
        for direction, (go, target) in enumerate(((gox, east), (gop, plus), (gom, minus))):
            @pl.when(go)
            def _(direction=direction, target=target):
                pltpu.make_async_remote_copy(
                    src_ref=kv.at[who, b], dst_ref=kv.at[who, b],
                    send_sem=ssem.at[step, direction], recv_sem=rsem.at[who, b],
                    device_id=target, device_id_type=MESH).start()

    def handed(step, who, gox, gop, gom):
        for direction, go in enumerate((gox, gop, gom)):
            @pl.when(go)
            def _(direction=direction):
                pltpu.make_async_copy(kv.at[who], kv.at[who], ssem.at[step, direction]).wait()

    own = (x < 3, y < 3, y == 0)

    def quarter(who, target, number):
        return pltpu.make_async_remote_copy(
            src_ref=kv.at[who, 3], dst_ref=kv.at[who, 3],
            send_sem=qtr.at[number], recv_sem=rsem.at[who, 3],
            device_id=target, device_id_type=MESH)

    def block_wait(sem):
        pltpu.make_async_copy(kv.at[0, 0], kv.at[0, 0], sem).wait()

    def features(who, b):
        flip = jnp.transpose(kv[who, b, HALF:, :].astype(jnp.float32)[:8])
        for p, size in ((0, D), (1, ROWS - D)):
            feat[pl.ds(pl.multiple_of(b * ROWS + p * D, 16), size), :] = jnp.where(
                flip[:size, p:p + 1] == lanes[:size], 0.0, -FAR).astype(jnp.bfloat16)

    def scores(r0, keys):
        return lax.dot_general(qaug[pl.ds(r0, SUB), :], keys, (((1,), (1,)), ((), ())),
                               preferred_element_type=jnp.float32)

    def finish(r0, sc, vals, start):
        here = pl.ds(r0, SUB)
        n = sc.shape[1]
        peak = jnp.broadcast_to(jnp.max(sc, axis=1, keepdims=True) * SCALE, (SUB, D))
        if not start:
            old = top[here, :]
            peak = jnp.maximum(old, peak)
        parts = []
        for j in range(0, n, D):
            w = min(D, n - j)
            parts.append(jnp.exp2(sc[:, j:j + w] * SCALE - peak[:, :w]).astype(jnp.bfloat16))
        weights = jnp.concatenate(parts, axis=1)
        out = jnp.dot(weights, vals, preferred_element_type=jnp.float32)
        if start:
            acc[here, :] = out
        else:
            factor = jnp.exp2(old - peak)
            acc[here, :D] = acc[here, :D] * factor + out[:, :D]
            acc[here, D:] = acc[here, D:] * factor + out[:, D:]
        top[here, :] = peak

    def attend(r, who, blocks, start, unroll):
        def keys():
            k = jnp.concatenate([kv[who, b, :ROWS, :] for b in blocks], axis=0)
            f = jnp.concatenate([feat[pl.ds(pl.multiple_of(b * ROWS, 16), ROWS), :] for b in blocks], axis=0)
            return jnp.concatenate([k, f], axis=1)

        def vals():
            v = jnp.concatenate([kv[who, b, ROWS:HALF, :] for b in blocks], axis=0)
            return jnp.concatenate([v, ones[:len(blocks) * ROWS, :]], axis=1)

        sc = scores(r, keys())
        for u in range(unroll):
            here = r + u * SUB
            nxt = scores(here + SUB, keys()) if u + 1 < unroll else None
            if start:
                shape = (SUB, len(blocks) * ROWS)
                row = here + lax.broadcasted_iota(jnp.int32, shape, 0)
                when = lax.broadcasted_iota(jnp.int32, shape, 1)
                sc = jnp.where(when * GROUP <= row, sc, -FAR)
            finish(here, sc, vals(), start)
            sc = nxt

    def sweep(who, blocks, start, count, unroll):
        def body(t, carry):
            attend(pl.multiple_of(t * (SUB * unroll), SUB * unroll), who, blocks, start, unroll)
            return carry

        lax.fori_loop(0, count // (SUB * unroll), body, 0)

    wait_rows(lsem.at[0], 2 * PIECE)
    wait_rows(zrecv.at[block], 6 * PIECE)
    hands(0, col, block, *own)
    block_wait(zrecv.at[order(1)])
    hands(0, col, order(1), *own)
    qlocal.wait()
    qcopy.wait_recv()
    for b in range(2):
        features(col, 2 * zh + b)
    sweep(col, (2 * zh, 2 * zh + 1), True, M, 2)

    for t in (2, 3):
        block_wait(zrecv.at[order(t)])
        hands(0, col, order(t), *own)

    def step_of(k):
        back = pick(BACK, y, k)
        who = (x - back) * 4 + pick(LANE, y, k)
        there = x >= back
        gox = there & (pick(GOX, y, k) > 0) & (x < 3)
        gop = there & (pick(GOP, y, k) > 0)
        gom = there & (pick(GOM, y, k) > 0)
        lone = there & (zh == 0) & (back == 2) & (who % 4 == y) & ((y < 3) | (x == 2))
        return who, there, gox, gop, gom, lone

    def onward(k, t):
        who, there, gox, gop, gom, lone = step_of(k)
        b = order(t)

        @pl.when(gox | gop | gom | lone)
        def _():
            block_wait(rsem.at[who, b])
            hands(k + 1, who, b, gox, gop, gom)

            @pl.when(lone & (b == 3) & (y < 3))
            def _():
                quarter(who, plus, 0).start()

            @pl.when(lone & (b == 3) & (y == 3))
            def _():
                quarter(who, east, 0).start()

    @pl.when(zh == 1)
    def _():
        for b in range(2):
            features(col, b)

    def rest(t, carry):
        onward(0, t)

        @pl.when(zh == 1)
        def _():
            attend(pl.multiple_of(t * (M // 4), SUB), col, (0, 1), False, M // 4 // SUB)

        return carry

    lax.fori_loop(0, 4, rest, 0)

    def step(k, carry):
        who, there, gox, gop, gom, lone = step_of(k)

        @pl.when(there & jnp.logical_not(gox | gop | gom | lone))
        def _():
            for b in range(4):
                block_wait(rsem.at[who, b])

        @pl.when(there)
        def _():
            for b in range(4):
                features(who, b)

        def part(t, carry):
            onward(k + 1, t)

            @pl.when(there)
            def _():
                attend(pl.multiple_of(t * (M // 4), SUB), who, (0, 1, 2, 3), False, M // 4 // SUB)

            return carry

        return lax.fori_loop(0, 4, part, carry)

    lax.fori_loop(0, STEPS, step, 0)

    corner = (zh == 0) & (x == 3)

    @pl.when(corner & (y == 3))
    def _():
        block_wait(rsem.at[3, 3])
        quarter(3, plus, 1).start()

    @pl.when(((zh == 0) & (x >= 2) & (y >= 1)) | (corner & (y == 0)))
    def _():
        who = col - 9
        block_wait(rsem.at[who, 3])
        features(who, 3)
        sweep(who, (3,), False, MC, 2)

    def result(b, slot):
        def body(t, carry):
            here = pl.ds(pl.multiple_of(b * MC + t * 256, 256), 256)
            obuf[slot, pl.ds(t * 256, 256), :] = (acc[here, :D] / acc[here, D:]).astype(jnp.bfloat16)
            return carry

        lax.fori_loop(0, MC // 256, body, 0)

    result(1 - c, c + 2)
    ocopy = pltpu.make_async_remote_copy(
        src_ref=obuf.at[c + 2], dst_ref=obuf.at[c],
        send_sem=osend, recv_sem=orecv, device_id=sibling, device_id_type=MESH)
    ocopy.start()
    result(c, c)
    ocopy.wait_recv()

    def join(t, carry):
        halves = [obuf[which, pl.ds(t * 128, 128), :].astype(jnp.float32).reshape(16, 8, D) for which in range(2)]
        o_ref[pl.ds(t * 256, 256), :] = jnp.concatenate(halves, axis=1).reshape(256, D).astype(jnp.bfloat16)
        return carry

    lax.fori_loop(0, ROWS // 16, join, 0)

    ocopy.wait_send()
    qcopy.wait_send()
    wait_rows(zsend.at[0], 14 * PIECE + 16)
    pltpu.make_async_copy(kv.at[0, pl.ds(0, 2)], kv.at[0, pl.ds(0, 2)], zsend.at[1]).wait()
    handed(0, col, *own)

    def drain(k, carry):
        who, there, gox, gop, gom, lone = step_of(k)
        handed(k + 1, who, gox, gop, gom)

        @pl.when(lone)
        def _():
            block_wait(qtr.at[0])

        return carry

    lax.fori_loop(0, STEPS, drain, 0)

    @pl.when(corner & (y == 3))
    def _():
        block_wait(qtr.at[1])


def per_device(queries, keys, values, doc_ids):
    bf, f32 = jnp.bfloat16, jnp.float32
    dma = pltpu.SemaphoreType.DMA
    vmem = pl.BlockSpec(memory_space=pltpu.VMEM)
    out = pl.pallas_call(
        kernel,
        out_shape=jax.ShapeDtypeStruct((ROWS * 16, D), bf),
        in_specs=[vmem] * 4,
        out_specs=vmem,
        scratch_shapes=[
            pltpu.VMEM((8 * PIECE, D), f32),
            pltpu.VMEM((8, 2, PIECE, D), bf),
            pltpu.VMEM((16, 4, CHUNK, D), bf),
            pltpu.VMEM((2, MC, 2 * D), bf),
            pltpu.VMEM((M, 2 * D), bf),
            pltpu.VMEM((KEYS, D), bf),
            pltpu.VMEM((KEYS, D), bf),
            pltpu.VMEM((M, D), f32),
            pltpu.VMEM((M, 2 * D), f32),
            pltpu.VMEM((4, MC, D), bf),
            dma((2,)), dma((4,)), dma((2,)), dma, dma, dma, dma,
            dma((STEPS + 1, 3)), dma((16, 4)), dma((2,)),
        ],
        compiler_params=pltpu.CompilerParams(
            collective_id=0, has_side_effects=True, vmem_limit_bytes=56 * 1024 * 1024),
    )(queries.reshape(ROWS * 16, D), keys.reshape(8 * PIECE, D), values.reshape(8 * PIECE, D),
      doc_ids.reshape(1, ROWS))
    return out.reshape(ROWS, 16, D)


def solution(mesh):
    return jax.shard_map(
        per_device,
        mesh=mesh,
        in_specs=(
            P("seq", "head", None),
            P(("seq", "head"), None, None),
            P(("seq", "head"), None, None),
            P("seq"),
        ),
        out_specs=P("seq", "head", None),
        check_vma=False,
    )
```

```python
import functools
import math

import jax
import jax.numpy as jnp
from jax import lax
from jax.experimental import pallas as pl
from jax.experimental.pallas import tpu as pltpu
from jax.sharding import PartitionSpec as P

MESH = pl.DeviceIdType.MESH

ROWS = 192
PIECE = 48
GROUP = 8
D = 128
HALF = 2 * ROWS
CHUNK = HALF + 16
KEYS = 2 * HALF
M = 2 * ROWS * GROUP
MC = ROWS * GROUP
SUB = 768
FAR = 2.0**20
SCALE = (1.0 / math.sqrt(D)) * math.log2(math.e)

PLAN = (
    ((1, 0, 1, 1, 1), (1, 1, 0, 0, 1), (1, 3, 0, 1, 0), (2, 0, 0, 0, 0),
     (1, 2, 0, 0, 0), (2, 1, 0, 0, 0), (2, 3, 0, 0, 0), (2, 2, 0, 0, 0)),
    ((0, 0, 0, 1, 0), (1, 1, 1, 1, 1), (1, 0, 0, 0, 0), (1, 2, 0, 0, 0),
     (2, 1, 0, 0, 1), (1, 3, 0, 0, 0), (2, 2, 0, 0, 1), (2, 3, 0, 0, 0)),
    ((0, 1, 0, 1, 0), (1, 2, 1, 1, 1), (0, 0, 0, 0, 0), (1, 1, 0, 0, 0),
     (1, 3, 0, 0, 0), (2, 2, 0, 0, 1), (1, 0, 0, 0, 0), (2, 3, 0, 0, 1)),
    ((0, 2, 0, 0, 0), (0, 0, 0, 0, 0), (1, 3, 1, 1, 1), (0, 1, 0, 0, 0),
     (1, 2, 0, 1, 0), (1, 0, 0, 0, 1), (2, 3, 0, 1, 1), (1, 1, 0, 0, 0)),
)
STEPS = len(PLAN[0])

ORDER = (
    (0, 1, 4, 8, 2, 5, 9, 3, 32, 33, 6, 10, 7, 36, 37, 11, 40, 41, 12, 13, 14, 15, 44, 45, 52, 53, 56, 57, 48, 49, 60, 61),
    (0, 4, 1, 5, 16, 2, 6, 3, 7, 24, 32, 33, 17, 36, 37, 18, 44, 19, 25, 45, 48, 49, 26, 40, 41, 27, 56, 57, 52, 53, 60, 61),
    (0, 4, 1, 5, 20, 6, 2, 7, 36, 37, 3, 21, 28, 32, 33, 22, 23, 48, 49, 52, 53, 29, 30, 40, 41, 44, 45, 31, 60, 61, 56, 57),
    (8, 9, 20, 24, 10, 16, 11, 36, 37, 21, 25, 40, 41, 26, 32, 17, 22, 27, 33, 56, 18, 57, 23, 52, 53, 19, 48, 49, 44, 45, 60, 61),
)


def packed(field):
    return [sum(step[field] << (2 * k) for k, step in enumerate(lane)) for lane in PLAN]


BACK, LANE, GOX, GOP, GOM = (packed(f) for f in range(5))


def pick(table, y, k):
    value = jnp.int32(table[3])
    for lane in range(3):
        value = jnp.where(y == lane, jnp.int32(table[lane]), value)
    return lax.shift_right_logical(value, 2 * k) & 3


def plane(bit):
    words = [sum(((op >> bit) & 1) << i for i, op in enumerate(lane)) for lane in ORDER]
    return [w - (1 << 32) if w >= 1 << 31 else w for w in words]


PLANES = [plane(bit) for bit in range(6)]


def fetch(y, i):
    value = 0
    for bit, words in enumerate(PLANES):
        word = jnp.int32(words[3])
        for lane in range(3):
            word = jnp.where(y == lane, jnp.int32(words[lane]), word)
        value = value + (lax.shift_right_logical(word, i) & 1) * (1 << bit)
    return value


def kernel(q_ref, k_ref, v_ref, id_ref, o_ref,
           wide, snd, kv, qst, qaug, feat, ones, top, acc, obuf,
           zsend, zrecv, lsem, qsend, qrecv, osend, orecv, ssem, rsem, qtr):
    s = lax.axis_index("seq")
    g = lax.axis_index("head")
    x, y, zh, c = s // 16, (s // 4) % 4, (s // 2) % 2, s % 2
    col = s // 4
    low = s % 4

    def at(xx, yy):
        return ((xx * 4 + yy) * 4 + low, g)

    def inside(dz, dc, dg):
        return (col * 4 + ((zh + dz) % 2) * 2 + (c + dc) % 2, (g + dg) % 4)

    sibling = inside(0, 1, 0)
    east = at((x + 1) % 4, y)
    plus = at(x, (y + 1) % 4)
    minus = at(x, (y + 3) % 4)
    others = [(dz, dc, dg) for dz in (0, 1) for dg in (0, 1, 3, 2) for dc in (0, 1) if dz or dc or dg]

    barrier = pltpu.get_barrier_semaphore()
    peers = [inside(*o) for o in others] + [east, at((x + 3) % 4, y), plus, minus]
    for peer in peers:
        pl.semaphore_signal(barrier, inc=1, device_id=peer, device_id_type=MESH)

    for which, ref in enumerate((k_ref, v_ref)):
        wide[...] = ref[...].astype(jnp.float32)
        for h in range(8):
            snd[h, which] = wide[pl.ds(h, PIECE, stride=8), :].astype(jnp.bfloat16)

    ids = id_ref[...].astype(jnp.float32)
    first = ids[:, :D]
    second = jnp.concatenate([ids[:, D:], jnp.zeros((1, 2 * D - ROWS), jnp.float32)], axis=1)
    tile = jnp.concatenate([first, second, jnp.zeros((14, D), jnp.float32)], axis=0)
    block = 2 * zh + c
    kv[col, block, HALF:, :] = tile.astype(jnp.bfloat16)

    pl.semaphore_wait(barrier, len(peers))

    spot = pl.multiple_of(PIECE * g, 16)
    for o in others:
        dz, dc, dg = o
        head = 2 * ((g + dg) % 4) + (c + dc) % 2
        for which in range(2):
            pltpu.make_async_remote_copy(
                src_ref=snd.at[head, which],
                dst_ref=kv.at[col, block, pl.ds(spot + which * ROWS, PIECE)],
                send_sem=zsend.at[dz], recv_sem=zrecv.at[block],
                device_id=inside(*o), device_id_type=MESH).start()
        if dg == 0:
            pltpu.make_async_remote_copy(
                src_ref=kv.at[col, block, pl.ds(HALF, 16)], dst_ref=kv.at[col, block, pl.ds(HALF, 16)],
                send_sem=zsend.at[dz], recv_sem=zrecv.at[block],
                device_id=inside(*o), device_id_type=MESH).start()
    for which in range(2):
        pltpu.make_async_copy(snd.at[2 * g + c, which], kv.at[col, block, pl.ds(spot + which * ROWS, PIECE)],
                              lsem.at[0]).start()

    def wait_rows(sem, n):
        pltpu.make_async_copy(feat.at[pl.ds(0, n)], feat.at[pl.ds(0, n)], sem).wait()

    turned = jnp.transpose(tile[:8])
    lanes = lax.broadcasted_iota(jnp.int32, (D, D), 1).astype(jnp.float32)
    for part, size in ((0, D), (1, ROWS - D)):
        hot = jnp.where(turned[:size, part:part + 1] == lanes[:size], 1.0, 0.0)
        hot = jnp.broadcast_to(hot[:, None, :], (size, GROUP, D)).reshape(size * GROUP, D)
        for which in range(2):
            qst[which, pl.ds(part * D * GROUP, size * GROUP), D:] = hot.astype(jnp.bfloat16)

    def split(t, carry):
        rows = q_ref[pl.ds(t * 16 * 16, 256), :].astype(jnp.float32).reshape(16, 16, D)
        for which in range(2):
            qst[which, pl.ds(t * 128, 128), :D] = (
                rows[:, 8 * which:8 * which + 8, :].reshape(128, D).astype(jnp.bfloat16))
        return carry

    lax.fori_loop(0, ROWS // 16, split, 0)
    base = pl.multiple_of(c * MC, MC)
    qcopy = pltpu.make_async_remote_copy(
        src_ref=qst.at[1 - c], dst_ref=qaug.at[pl.ds(base, MC)],
        send_sem=qsend, recv_sem=qrecv, device_id=sibling, device_id_type=MESH)
    qcopy.start()
    qlocal = pltpu.make_async_copy(qst.at[c], qaug.at[pl.ds(base, MC)], lsem.at[1])
    qlocal.start()
    ones[...] = jnp.ones_like(ones)

    def order(t):
        return 2 * ((zh + t // 2) % 2) + (c + t) % 2

    def hands(step, who, b, gox, gop, gom):
        for direction, (go, target) in enumerate(((gox, east), (gop, plus), (gom, minus))):
            @pl.when(go)
            def _(direction=direction, target=target):
                pltpu.make_async_remote_copy(
                    src_ref=kv.at[who, b], dst_ref=kv.at[who, b],
                    send_sem=ssem.at[step, direction], recv_sem=rsem.at[who, b],
                    device_id=target, device_id_type=MESH).start()

    def handed(step, who, gox, gop, gom):
        for direction, go in enumerate((gox, gop, gom)):
            @pl.when(go)
            def _(direction=direction):
                pltpu.make_async_copy(kv.at[who], kv.at[who], ssem.at[step, direction]).wait()

    own = (x < 3, y < 3, y == 0)

    def quarter(who, target, number):
        return pltpu.make_async_remote_copy(
            src_ref=kv.at[who, 3], dst_ref=kv.at[who, 3],
            send_sem=qtr.at[number], recv_sem=rsem.at[who, 3],
            device_id=target, device_id_type=MESH)

    def block_wait(sem):
        pltpu.make_async_copy(kv.at[0, 0], kv.at[0, 0], sem).wait()

    def features(who, b):
        flip = jnp.transpose(kv[who, b, HALF:, :].astype(jnp.float32)[:8])
        for p, size in ((0, D), (1, ROWS - D)):
            feat[pl.ds(pl.multiple_of(b * ROWS + p * D, 16), size), :] = jnp.where(
                flip[:size, p:p + 1] == lanes[:size], 0.0, -FAR).astype(jnp.bfloat16)

    def scores(r0, keys):
        return lax.dot_general(qaug[pl.ds(r0, SUB), :], keys, (((1,), (1,)), ((), ())),
                               preferred_element_type=jnp.float32)

    def finish(r0, sc, vals, start):
        here = pl.ds(r0, SUB)
        n = sc.shape[1]
        peak = jnp.broadcast_to(jnp.max(sc, axis=1, keepdims=True) * SCALE, (SUB, D))
        if not start:
            old = top[here, :]
            peak = jnp.maximum(old, peak)
        parts = []
        for j in range(0, n, D):
            w = min(D, n - j)
            parts.append(jnp.exp2(sc[:, j:j + w] * SCALE - peak[:, :w]).astype(jnp.bfloat16))
        weights = jnp.concatenate(parts, axis=1)
        out = jnp.dot(weights, vals, preferred_element_type=jnp.float32)
        if start:
            acc[here, :] = out
        else:
            factor = jnp.exp2(old - peak)
            acc[here, :D] = acc[here, :D] * factor + out[:, :D]
            acc[here, D:] = acc[here, D:] * factor + out[:, D:]
        top[here, :] = peak

    def attend(r, who, blocks, start, unroll):
        def keys():
            k = jnp.concatenate([kv[who, b, :ROWS, :] for b in blocks], axis=0)
            f = jnp.concatenate([feat[pl.ds(pl.multiple_of(b * ROWS, 16), ROWS), :] for b in blocks], axis=0)
            return jnp.concatenate([k, f], axis=1)

        def vals():
            v = jnp.concatenate([kv[who, b, ROWS:HALF, :] for b in blocks], axis=0)
            return jnp.concatenate([v, ones[:len(blocks) * ROWS, :]], axis=1)

        sc = scores(r, keys())
        for u in range(unroll):
            here = r + u * SUB
            nxt = scores(here + SUB, keys()) if u + 1 < unroll else None
            if start:
                shape = (SUB, len(blocks) * ROWS)
                row = here + lax.broadcasted_iota(jnp.int32, shape, 0)
                when = lax.broadcasted_iota(jnp.int32, shape, 1)
                sc = jnp.where(when * GROUP <= row, sc, -FAR)
            finish(here, sc, vals(), start)
            sc = nxt

    def sweep(who, blocks, start, count, unroll):
        def body(t, carry):
            attend(pl.multiple_of(t * (SUB * unroll), SUB * unroll), who, blocks, start, unroll)
            return carry

        lax.fori_loop(0, count // (SUB * unroll), body, 0)

    wait_rows(lsem.at[0], 2 * PIECE)
    wait_rows(zrecv.at[block], 6 * PIECE)
    hands(0, col, block, *own)
    block_wait(zrecv.at[order(1)])
    hands(0, col, order(1), *own)
    qlocal.wait()
    qcopy.wait_recv()
    for b in range(2):
        features(col, 2 * zh + b)
    sweep(col, (2 * zh, 2 * zh + 1), True, M, 2)

    for t in (2, 3):
        block_wait(zrecv.at[order(t)])
        hands(0, col, order(t), *own)

    def step_of(k):
        back = pick(BACK, y, k)
        who = (x - back) * 4 + pick(LANE, y, k)
        there = x >= back
        gox = there & (pick(GOX, y, k) > 0) & (x < 3)
        gop = there & (pick(GOP, y, k) > 0)
        gom = there & (pick(GOM, y, k) > 0)
        lone = there & (zh == 0) & (back == 2) & (who % 4 == y) & ((y < 3) | (x == 2))
        return who, there, gox, gop, gom, lone

    def onward(k, t):
        who, there, gox, gop, gom, lone = step_of(k)
        b = order(t)

        @pl.when(gox | gop | gom | lone)
        def _():
            block_wait(rsem.at[who, b])
            hands(k + 1, who, b, gox, gop, gom)

            @pl.when(lone & (b == 3) & (y < 3))
            def _():
                quarter(who, plus, 0).start()

            @pl.when(lone & (b == 3) & (y == 3))
            def _():
                quarter(who, east, 0).start()

    @pl.when(zh == 1)
    def _():
        for b in range(2):
            features(col, b)

    def rest(t, carry):
        @pl.when(zh == 1)
        def _():
            attend(pl.multiple_of(t * (M // 2), SUB), col, (0, 1), False, M // 2 // SUB)

        return carry

    lax.fori_loop(0, 2, rest, 0)

    def work(k, t):
        who, there, gox, gop, gom, lone = step_of(k)

        @pl.when(there & (t == 0) & jnp.logical_not(gox | gop | gom | lone))
        def _():
            for b in range(4):
                block_wait(rsem.at[who, b])

        @pl.when(there & (t == 0))
        def _():
            for b in range(4):
                features(who, b)

        @pl.when(there)
        def _():
            attend(pl.multiple_of(t * (M // 2), SUB), who, (0, 1, 2, 3), False, M // 2 // SUB)

    def turn(i, carry):
        op = fetch(y, i)
        k, t = (op // 4) % 8, op % 4

        @pl.when(op < 32)
        def _():
            onward(k, t)

        @pl.when(op >= 32)
        def _():
            work(k, t)

        return carry

    lax.fori_loop(0, 32, turn, 0)

    corner = (zh == 0) & (x == 3)

    @pl.when(corner & (y == 3))
    def _():
        block_wait(rsem.at[3, 3])
        quarter(3, plus, 1).start()

    @pl.when(((zh == 0) & (x >= 2) & (y >= 1)) | (corner & (y == 0)))
    def _():
        who = col - 9
        block_wait(rsem.at[who, 3])
        features(who, 3)
        sweep(who, (3,), False, MC, 2)

    def result(b, slot):
        def body(t, carry):
            here = pl.ds(pl.multiple_of(b * MC + t * 256, 256), 256)
            obuf[slot, pl.ds(t * 256, 256), :] = (acc[here, :D] / acc[here, D:]).astype(jnp.bfloat16)
            return carry

        lax.fori_loop(0, MC // 256, body, 0)

    result(1 - c, c + 2)
    ocopy = pltpu.make_async_remote_copy(
        src_ref=obuf.at[c + 2], dst_ref=obuf.at[c],
        send_sem=osend, recv_sem=orecv, device_id=sibling, device_id_type=MESH)
    ocopy.start()
    result(c, c)
    ocopy.wait_recv()

    def join(t, carry):
        halves = [obuf[which, pl.ds(t * 128, 128), :].astype(jnp.float32).reshape(16, 8, D) for which in range(2)]
        o_ref[pl.ds(t * 256, 256), :] = jnp.concatenate(halves, axis=1).reshape(256, D).astype(jnp.bfloat16)
        return carry

    lax.fori_loop(0, ROWS // 16, join, 0)

    ocopy.wait_send()
    qcopy.wait_send()
    wait_rows(zsend.at[0], 14 * PIECE + 16)
    pltpu.make_async_copy(kv.at[0, pl.ds(0, 2)], kv.at[0, pl.ds(0, 2)], zsend.at[1]).wait()
    handed(0, col, *own)

    def drain(k, carry):
        who, there, gox, gop, gom, lone = step_of(k)
        handed(k + 1, who, gox, gop, gom)

        @pl.when(lone)
        def _():
            block_wait(qtr.at[0])

        return carry

    lax.fori_loop(0, STEPS, drain, 0)

    @pl.when(corner & (y == 3))
    def _():
        block_wait(qtr.at[1])


def per_device(queries, keys, values, doc_ids):
    bf, f32 = jnp.bfloat16, jnp.float32
    dma = pltpu.SemaphoreType.DMA
    vmem = pl.BlockSpec(memory_space=pltpu.VMEM)
    out = pl.pallas_call(
        kernel,
        out_shape=jax.ShapeDtypeStruct((ROWS * 16, D), bf),
        in_specs=[vmem] * 4,
        out_specs=vmem,
        scratch_shapes=[
            pltpu.VMEM((8 * PIECE, D), f32),
            pltpu.VMEM((8, 2, PIECE, D), bf),
            pltpu.VMEM((16, 4, CHUNK, D), bf),
            pltpu.VMEM((2, MC, 2 * D), bf),
            pltpu.VMEM((M, 2 * D), bf),
            pltpu.VMEM((KEYS, D), bf),
            pltpu.VMEM((KEYS, D), bf),
            pltpu.VMEM((M, D), f32),
            pltpu.VMEM((M, 2 * D), f32),
            pltpu.VMEM((4, MC, D), bf),
            dma((2,)), dma((4,)), dma((2,)), dma, dma, dma, dma,
            dma((STEPS + 1, 3)), dma((16, 4)), dma((2,)),
        ],
        compiler_params=pltpu.CompilerParams(
            collective_id=0, has_side_effects=True, vmem_limit_bytes=56 * 1024 * 1024),
    )(queries.reshape(ROWS * 16, D), keys.reshape(8 * PIECE, D), values.reshape(8 * PIECE, D),
      doc_ids.reshape(1, ROWS))
    return out.reshape(ROWS, 16, D)


def solution(mesh):
    return jax.shard_map(
        per_device,
        mesh=mesh,
        in_specs=(
            P("seq", "head", None),
            P(("seq", "head"), None, None),
            P(("seq", "head"), None, None),
            P("seq"),
        ),
        out_specs=P("seq", "head", None),
        check_vma=False,
    )
```

```python
import functools
import math

import jax
import jax.numpy as jnp
from jax import lax
from jax.experimental import pallas as pl
from jax.experimental.pallas import tpu as pltpu
from jax.sharding import PartitionSpec as P

MESH = pl.DeviceIdType.MESH

ROWS = 192
PIECE = 48
GROUP = 8
D = 128
HALF = 2 * ROWS
CHUNK = HALF + 16
KEYS = 2 * HALF
M = 2 * ROWS * GROUP
MC = ROWS * GROUP
SUB = 768
FAR = 2.0**20
SCALE = (1.0 / math.sqrt(D)) * math.log2(math.e)

PLAN = (
    ((1, 0, 1, 1, 1), (1, 1, 0, 0, 1), (1, 3, 0, 1, 0), (2, 0, 0, 0, 0),
     (1, 2, 0, 0, 0), (2, 1, 0, 0, 0), (2, 3, 0, 0, 0), (2, 2, 0, 0, 0)),
    ((0, 0, 0, 1, 0), (1, 1, 1, 1, 1), (1, 0, 0, 0, 0), (1, 2, 0, 0, 0),
     (2, 1, 0, 0, 1), (1, 3, 0, 0, 0), (2, 2, 0, 0, 1), (2, 3, 0, 0, 0)),
    ((0, 1, 0, 1, 0), (1, 2, 1, 1, 1), (0, 0, 0, 0, 0), (1, 1, 0, 0, 0),
     (1, 3, 0, 0, 0), (2, 2, 0, 0, 1), (1, 0, 0, 0, 0), (2, 3, 0, 0, 1)),
    ((0, 2, 0, 0, 0), (0, 0, 0, 0, 0), (1, 3, 1, 1, 1), (0, 1, 0, 0, 0),
     (1, 2, 0, 1, 0), (1, 0, 0, 0, 1), (2, 3, 0, 1, 1), (1, 1, 0, 0, 0)),
)
STEPS = len(PLAN[0])
RELAY = 22

ORDER = (
    (0, 1, 34, 35, 64, 4, 8, 5, 9, 258, 2, 12, 13, 326, 3, 282, 6, 10, 14, 15, 455, 7, 11, 309, 398, 445, 415),
    (0, 4, 1, 5, 34, 258, 35, 64, 16, 17, 326, 2, 6, 24, 3, 7, 25, 385, 18, 316, 19, 377, 26, 421, 27, 475, 495),
    (0, 4, 1, 5, 34, 258, 35, 64, 20, 21, 394, 6, 7, 28, 323, 2, 22, 364, 3, 23, 29, 283, 489, 30, 31, 343, 509),
    (8, 9, 34, 258, 35, 64, 20, 24, 16, 21, 25, 330, 10, 454, 11, 17, 309, 26, 27, 385, 18, 22, 478, 19, 23, 411, 383),
)


def packed(field):
    return [sum(step[field] << (2 * k) for k, step in enumerate(lane)) for lane in PLAN]


BACK, LANE, GOX, GOP, GOM = (packed(f) for f in range(5))


def pick(table, y, k):
    value = jnp.int32(table[3])
    for lane in range(3):
        value = jnp.where(y == lane, jnp.int32(table[lane]), value)
    return lax.shift_right_logical(value, 2 * k) & 3


def plane(bit):
    words = [sum(((op >> bit) & 1) << i for i, op in enumerate(lane)) for lane in ORDER]
    return [w - (1 << 32) if w >= 1 << 31 else w for w in words]


PLANES = [plane(bit) for bit in range(9)]


def fetch(y, i):
    value = 0
    for bit, words in enumerate(PLANES):
        word = jnp.int32(words[3])
        for lane in range(3):
            word = jnp.where(y == lane, jnp.int32(words[lane]), word)
        value = value + (lax.shift_right_logical(word, i) & 1) * (1 << bit)
    return value


def kernel(q_ref, k_ref, v_ref, id_ref, o_ref,
           wide, snd, kv, qst, qaug, feat, ones, top, acc, obuf,
           zsend, zrecv, lsem, qsend, qrecv, osend, orecv, ssem, rsem, qtr):
    s = lax.axis_index("seq")
    g = lax.axis_index("head")
    x, y, zh, c = s // 16, (s // 4) % 4, (s // 2) % 2, s % 2
    col = s // 4
    low = s % 4

    def at(xx, yy):
        return ((xx * 4 + yy) * 4 + low, g)

    def inside(dz, dc, dg):
        return (col * 4 + ((zh + dz) % 2) * 2 + (c + dc) % 2, (g + dg) % 4)

    sibling = inside(0, 1, 0)
    east = at((x + 1) % 4, y)
    plus = at(x, (y + 1) % 4)
    minus = at(x, (y + 3) % 4)
    others = [(dz, dc, dg) for dz in (0, 1) for dg in (0, 1, 3, 2) for dc in (0, 1) if dz or dc or dg]

    barrier = pltpu.get_barrier_semaphore()
    peers = [inside(*o) for o in others] + [east, at((x + 3) % 4, y), plus, minus]
    for peer in peers:
        pl.semaphore_signal(barrier, inc=1, device_id=peer, device_id_type=MESH)

    for which, ref in enumerate((k_ref, v_ref)):
        wide[...] = ref[...].astype(jnp.float32)
        for h in range(8):
            snd[h, which] = wide[pl.ds(h, PIECE, stride=8), :].astype(jnp.bfloat16)

    ids = id_ref[...].astype(jnp.float32)
    first = ids[:, :D]
    second = jnp.concatenate([ids[:, D:], jnp.zeros((1, 2 * D - ROWS), jnp.float32)], axis=1)
    tile = jnp.concatenate([first, second, jnp.zeros((14, D), jnp.float32)], axis=0)
    block = 2 * zh + c
    kv[col, block, HALF:, :] = tile.astype(jnp.bfloat16)

    pl.semaphore_wait(barrier, len(peers))

    spot = pl.multiple_of(PIECE * g, 16)

    def spread(plane):
        for o in others:
            dz, dc, dg = o
            if dz != plane:
                continue
            head = 2 * ((g + dg) % 4) + (c + dc) % 2
            for which in range(2):
                pltpu.make_async_remote_copy(
                    src_ref=snd.at[head, which],
                    dst_ref=kv.at[col, block, pl.ds(spot + which * ROWS, PIECE)],
                    send_sem=zsend.at[dz], recv_sem=zrecv.at[block],
                    device_id=inside(*o), device_id_type=MESH).start()
            if dg == 0:
                pltpu.make_async_remote_copy(
                    src_ref=kv.at[col, block, pl.ds(HALF, 16)], dst_ref=kv.at[col, block, pl.ds(HALF, 16)],
                    send_sem=zsend.at[dz], recv_sem=zrecv.at[block],
                    device_id=inside(*o), device_id_type=MESH).start()

    spread(0)
    for which in range(2):
        pltpu.make_async_copy(snd.at[2 * g + c, which], kv.at[col, block, pl.ds(spot + which * ROWS, PIECE)],
                              lsem.at[0]).start()

    def wait_rows(sem, n):
        pltpu.make_async_copy(feat.at[pl.ds(0, n)], feat.at[pl.ds(0, n)], sem).wait()

    turned = jnp.transpose(tile[:8])
    lanes = lax.broadcasted_iota(jnp.int32, (D, D), 1).astype(jnp.float32)
    for part, size in ((0, D), (1, ROWS - D)):
        hot = jnp.where(turned[:size, part:part + 1] == lanes[:size], 1.0, 0.0)
        hot = jnp.broadcast_to(hot[:, None, :], (size, GROUP, D)).reshape(size * GROUP, D)
        for which in range(2):
            qst[which, pl.ds(part * D * GROUP, size * GROUP), D:] = hot.astype(jnp.bfloat16)

    def split(t, carry):
        rows = q_ref[pl.ds(t * 16 * 16, 256), :].astype(jnp.float32).reshape(16, 16, D)
        for which in range(2):
            qst[which, pl.ds(t * 128, 128), :D] = (
                rows[:, 8 * which:8 * which + 8, :].reshape(128, D).astype(jnp.bfloat16))
        return carry

    lax.fori_loop(0, ROWS // 16, split, 0)
    base = pl.multiple_of(c * MC, MC)
    qcopy = pltpu.make_async_remote_copy(
        src_ref=qst.at[1 - c], dst_ref=qaug.at[pl.ds(base, MC)],
        send_sem=qsend, recv_sem=qrecv, device_id=sibling, device_id_type=MESH)
    qcopy.start()
    qlocal = pltpu.make_async_copy(qst.at[c], qaug.at[pl.ds(base, MC)], lsem.at[1])
    qlocal.start()
    spread(1)
    ones[...] = jnp.ones_like(ones)

    def order(t):
        return 2 * ((zh + t // 2) % 2) + (c + t) % 2

    def hands(step, who, b, gox, gop, gom):
        for direction, (go, target) in enumerate(((gox, east), (gop, plus), (gom, minus))):
            @pl.when(go)
            def _(direction=direction, target=target):
                pltpu.make_async_remote_copy(
                    src_ref=kv.at[who, b], dst_ref=kv.at[who, b],
                    send_sem=ssem.at[step, direction], recv_sem=rsem.at[who, b],
                    device_id=target, device_id_type=MESH).start()

    def handed(step, who, gox, gop, gom):
        for direction, go in enumerate((gox, gop, gom)):
            @pl.when(go)
            def _(direction=direction):
                pltpu.make_async_copy(kv.at[who], kv.at[who], ssem.at[step, direction]).wait()

    own = (x < 3, y < 3, y == 0)

    def quarter(who, target, number):
        return pltpu.make_async_remote_copy(
            src_ref=kv.at[who, 3], dst_ref=kv.at[who, 3],
            send_sem=qtr.at[number], recv_sem=rsem.at[who, 3],
            device_id=target, device_id_type=MESH)

    def block_wait(sem):
        pltpu.make_async_copy(kv.at[0, 0], kv.at[0, 0], sem).wait()

    def features(i, who, b, near):
        flip = jnp.transpose(kv[who, b, HALF:, :].astype(jnp.float32)[:8])
        for p, size in ((0, D), (1, ROWS - D)):
            feat[pl.ds(i * ROWS + p * D, size), :] = jnp.where(
                flip[:size, p:p + 1] == lanes[:size], near, -FAR).astype(jnp.bfloat16)

    def scores(r0, keys):
        return lax.dot_general(qaug[pl.ds(r0, SUB), :], keys, (((1,), (1,)), ((), ())),
                               preferred_element_type=jnp.float32)

    def finish(r0, sc, vals, start):
        here = pl.ds(r0, SUB)
        n = sc.shape[1]
        peak = jnp.broadcast_to(jnp.max(sc, axis=1, keepdims=True) * SCALE, (SUB, D))
        if not start:
            old = top[here, :]
            peak = jnp.maximum(old, peak)
        parts = []
        for j in range(0, n, D):
            w = min(D, n - j)
            parts.append(jnp.exp2(sc[:, j:j + w] * SCALE - peak[:, :w]).astype(jnp.bfloat16))
        weights = jnp.concatenate(parts, axis=1)
        out = jnp.dot(weights, vals, preferred_element_type=jnp.float32)
        if start:
            acc[here, :] = out
        else:
            factor = jnp.exp2(old - peak)
            acc[here, :D] = acc[here, :D] * factor + out[:, :D]
            acc[here, D:] = acc[here, D:] * factor + out[:, D:]
        top[here, :] = peak

    def attend(r, blocks, start, unroll):
        n = len(blocks) * ROWS

        def keys():
            k = jnp.concatenate([kv[who, b, :ROWS, :] for who, b in blocks], axis=0)
            return jnp.concatenate([k, feat[:n, :]], axis=1)

        def vals():
            v = jnp.concatenate([kv[who, b, ROWS:HALF, :] for who, b in blocks], axis=0)
            return jnp.concatenate([v, ones[:n, :]], axis=1)

        sc = scores(r, keys())
        for u in range(unroll):
            here = r + u * SUB
            nxt = scores(here + SUB, keys()) if u + 1 < unroll else None
            if start:
                shape = (SUB, n)
                row = here + lax.broadcasted_iota(jnp.int32, shape, 0)
                when = lax.broadcasted_iota(jnp.int32, shape, 1)
                sc = jnp.where(when * GROUP <= row, sc, -FAR)
            finish(here, sc, vals(), start)
            sc = nxt

    def sweep(blocks, nears, start, count, unroll):
        for i, ((who, b), near) in enumerate(zip(blocks, nears)):
            features(i, who, b, near)

        def body(t, carry):
            attend(pl.multiple_of(t * (SUB * unroll), SUB * unroll), blocks, start, unroll)
            return carry

        lax.fori_loop(0, count // (SUB * unroll), body, 0)

    wait_rows(lsem.at[0], 2 * PIECE)
    wait_rows(zrecv.at[block], 6 * PIECE)
    hands(0, col, block, *own)
    block_wait(zrecv.at[order(1)])
    hands(0, col, order(1), *own)
    qlocal.wait()
    qcopy.wait_recv()
    sweep([(col, 2 * zh), (col, 2 * zh + 1)], [0.0] * 2, True, M, 4)

    def step_of(k):
        back = pick(BACK, y, k)
        who = (x - back) * 4 + pick(LANE, y, k)
        there = x >= back
        gox = there & (pick(GOX, y, k) > 0) & (x < 3)
        gop = there & (pick(GOP, y, k) > 0)
        gom = there & (pick(GOM, y, k) > 0)
        lone = there & (zh == 0) & (back == 2) & (who % 4 == y) & ((y < 3) | (x == 2))
        return who, there, gox, gop, gom, lone

    def onward(k, t):
        who, there, gox, gop, gom, lone = step_of(k)
        b = order(t)

        @pl.when(gox | gop | gom | lone)
        def _():
            block_wait(rsem.at[who, b])
            hands(k + 1, who, b, gox, gop, gom)

            @pl.when(lone & (b == 3) & (y < 3))
            def _():
                quarter(who, plus, 0).start()

            @pl.when(lone & (b == 3) & (y == 3))
            def _():
                quarter(who, east, 0).start()

    corner = (zh == 0) & (x == 3)

    def turn(i, carry):
        op = fetch(y, i)

        @pl.when(op < 32)
        def _():
            onward(op // 4, op % 4)

        @pl.when((op >= 32) & (op < 64))
        def _():
            b = order(op % 4)
            block_wait(zrecv.at[b])
            hands(0, col, b, *own)

        @pl.when((op == 64) & (zh == 1))
        def _():
            sweep([(col, 0), (col, 1)], [0.0] * 2, False, M, 4)

        blocks, nears, present = [], [], []
        for pair in ((op % 256) // 16, op % 16):
            who, there, gox, gop, gom, lone = step_of(pair // 2)
            pairs = [order(2 * (pair % 2) + j) for j in range(2)]

            @pl.when((op >= 256) & there & jnp.logical_not(gox | gop | gom | lone))
            def _(who=who, pairs=pairs):
                for b in pairs:
                    block_wait(rsem.at[who, b])

            blocks += [(jnp.where(there, who, col), b) for b in pairs]
            nears += [jnp.where(there, 0.0, -FAR)] * 2
            present.append(there)

        @pl.when((op >= 256) & (present[0] | present[1]))
        def _():
            sweep(blocks, nears, False, M, 4)

        @pl.when((i == RELAY) & corner & (y == 3))
        def _():
            block_wait(rsem.at[3, 3])
            quarter(3, plus, 1).start()

        return carry

    lax.fori_loop(0, len(ORDER[0]), turn, 0)

    @pl.when(((zh == 0) & (x >= 2) & (y >= 1)) | (corner & (y == 0)))
    def _():
        who = col - 9
        block_wait(rsem.at[who, 3])
        sweep([(who, 3)], [0.0], False, MC, 2)

    def result(b, ref, slot):
        def body(t, carry):
            here = pl.ds(pl.multiple_of(b * MC + t * 256, 256), 256)
            ref[slot, pl.ds(t * 256, 256), :] = (acc[here, :D] / acc[here, D:]).astype(jnp.bfloat16)
            return carry

        lax.fori_loop(0, MC // 256, body, 0)

    result(1 - c, obuf, 0)
    ocopy = pltpu.make_async_remote_copy(
        src_ref=obuf.at[0], dst_ref=o_ref.at[c],
        send_sem=osend, recv_sem=orecv, device_id=sibling, device_id_type=MESH)
    ocopy.start()
    result(c, o_ref, c)
    ocopy.wait_recv()

    ocopy.wait_send()
    qcopy.wait_send()
    wait_rows(zsend.at[0], 14 * PIECE + 16)
    pltpu.make_async_copy(kv.at[0, pl.ds(0, 2)], kv.at[0, pl.ds(0, 2)], zsend.at[1]).wait()
    handed(0, col, *own)

    def drain(k, carry):
        who, there, gox, gop, gom, lone = step_of(k)
        handed(k + 1, who, gox, gop, gom)

        @pl.when(lone)
        def _():
            block_wait(qtr.at[0])

        return carry

    lax.fori_loop(0, STEPS, drain, 0)

    @pl.when(corner & (y == 3))
    def _():
        block_wait(qtr.at[1])


def per_device(queries, keys, values, doc_ids):
    bf, f32 = jnp.bfloat16, jnp.float32
    dma = pltpu.SemaphoreType.DMA
    vmem = pl.BlockSpec(memory_space=pltpu.VMEM)
    out = pl.pallas_call(
        kernel,
        out_shape=jax.ShapeDtypeStruct((2, MC, D), bf),
        in_specs=[vmem] * 4,
        out_specs=vmem,
        scratch_shapes=[
            pltpu.VMEM((8 * PIECE, D), f32),
            pltpu.VMEM((8, 2, PIECE, D), bf),
            pltpu.VMEM((16, 4, CHUNK, D), bf),
            pltpu.VMEM((2, MC, 2 * D), bf),
            pltpu.VMEM((M, 2 * D), bf),
            pltpu.VMEM((KEYS, D), bf),
            pltpu.VMEM((KEYS, D), bf),
            pltpu.VMEM((M, D), f32),
            pltpu.VMEM((M, 2 * D), f32),
            pltpu.VMEM((1, MC, D), bf),
            dma((2,)), dma((4,)), dma((2,)), dma, dma, dma, dma,
            dma((STEPS + 1, 3)), dma((16, 4)), dma((2,)),
        ],
        compiler_params=pltpu.CompilerParams(
            collective_id=0, has_side_effects=True, vmem_limit_bytes=56 * 1024 * 1024),
    )(queries.reshape(ROWS * 16, D), keys.reshape(8 * PIECE, D), values.reshape(8 * PIECE, D),
      doc_ids.reshape(1, ROWS))
    return jnp.swapaxes(out.reshape(2, ROWS, GROUP, D), 0, 1).reshape(ROWS, 2 * GROUP, D)


def solution(mesh):
    return jax.shard_map(
        per_device,
        mesh=mesh,
        in_specs=(
            P("seq", "head", None),
            P(("seq", "head"), None, None),
            P(("seq", "head"), None, None),
            P("seq"),
        ),
        out_specs=P("seq", "head", None),
        check_vma=False,
    )
```

```python
import functools
import math

import jax
import jax.numpy as jnp
from jax import lax
from jax.experimental import pallas as pl
from jax.experimental.pallas import tpu as pltpu
from jax.sharding import PartitionSpec as P

MESH = pl.DeviceIdType.MESH

ROWS = 192
PIECE = 48
GROUP = 8
D = 128
HALF = 2 * ROWS
CHUNK = HALF + 16
KEYS = 2 * HALF
M = 2 * ROWS * GROUP
MC = ROWS * GROUP
SUB = 768
FAR = 2.0**20
SCALE = (1.0 / math.sqrt(D)) * math.log2(math.e)

PLAN = (
    ((1, 0, 1, 1, 1), (1, 1, 0, 0, 1), (1, 3, 0, 1, 0), (2, 0, 0, 0, 0),
     (1, 2, 0, 0, 0), (2, 1, 0, 0, 0), (2, 3, 0, 0, 0), (2, 2, 0, 0, 0)),
    ((0, 0, 0, 1, 0), (1, 1, 1, 1, 1), (1, 0, 0, 0, 0), (1, 2, 0, 0, 0),
     (2, 1, 0, 0, 1), (1, 3, 0, 0, 0), (2, 2, 0, 0, 1), (2, 3, 0, 0, 0)),
    ((0, 1, 0, 1, 0), (1, 2, 1, 1, 1), (0, 0, 0, 0, 0), (1, 1, 0, 0, 0),
     (1, 3, 0, 0, 0), (2, 2, 0, 0, 1), (1, 0, 0, 0, 0), (2, 3, 0, 0, 1)),
    ((0, 2, 0, 0, 0), (0, 0, 0, 0, 0), (1, 3, 1, 1, 1), (0, 1, 0, 0, 0),
     (1, 2, 0, 1, 0), (1, 0, 0, 0, 1), (2, 3, 0, 1, 1), (1, 1, 0, 0, 0)),
)
STEPS = len(PLAN[0])
RELAY = 22
LATE = 21

ORDER = (
    (0, 1, 34, 35, 64, 4, 8, 5, 9, 258, 2, 12, 13, 326, 3, 282, 6, 10, 14, 15, 455, 7, 11, 309, 398, 445, 415),
    (0, 4, 1, 5, 34, 258, 35, 64, 16, 17, 326, 2, 6, 24, 3, 7, 25, 385, 18, 316, 19, 377, 26, 421, 27, 475, 495),
    (0, 4, 1, 5, 34, 258, 35, 64, 20, 21, 394, 6, 7, 28, 323, 2, 22, 364, 3, 23, 29, 283, 489, 30, 31, 343, 509),
    (8, 9, 34, 258, 35, 64, 20, 24, 16, 21, 25, 330, 10, 454, 11, 17, 309, 26, 27, 385, 18, 22, 478, 19, 23, 411, 383),
)


def packed(field):
    return [sum(step[field] << (2 * k) for k, step in enumerate(lane)) for lane in PLAN]


BACK, LANE, GOX, GOP, GOM = (packed(f) for f in range(5))


def by_lane(tables, y):
    words = []
    for table in tables:
        word = jnp.int32(table[3])
        for lane in range(3):
            word = jnp.where(y == lane, jnp.int32(table[lane]), word)
        words.append(word)
    return words


def pick(word, k):
    return lax.shift_right_logical(word, 2 * k) & 3


def plane(bit):
    words = [sum(((op >> bit) & 1) << i for i, op in enumerate(lane)) for lane in ORDER]
    return [w - (1 << 32) if w >= 1 << 31 else w for w in words]


PLANES = [plane(bit) for bit in range(9)]


def fetch(words, i):
    value = 0
    for bit, word in enumerate(words):
        value = value + (lax.shift_right_logical(word, i) & 1) * (1 << bit)
    return value


def kernel(q_ref, k_ref, v_ref, id_ref, o_ref,
           wide, snd, kv, qst, qaug, feat, ones, top, acc, obuf,
           zsend, zrecv, lsem, qsend, qrecv, osend, orecv, ssem, rsem, qtr):
    s = lax.axis_index("seq")
    g = lax.axis_index("head")
    x, y, zh, c = s // 16, (s // 4) % 4, (s // 2) % 2, s % 2
    col = s // 4
    low = s % 4

    def at(xx, yy):
        return ((xx * 4 + yy) * 4 + low, g)

    def inside(dz, dc, dg):
        return (col * 4 + ((zh + dz) % 2) * 2 + (c + dc) % 2, (g + dg) % 4)

    sibling = inside(0, 1, 0)
    east = at((x + 1) % 4, y)
    plus = at(x, (y + 1) % 4)
    minus = at(x, (y + 3) % 4)
    others = [(dz, dc, dg) for dz in (0, 1) for dc in (0, 1) for dg in (2, 1, 3, 0) if dz or dc or dg]

    barrier = pltpu.get_barrier_semaphore()
    peers = [inside(*o) for o in others] + [east, at((x + 3) % 4, y), plus, minus]
    for peer in peers:
        pl.semaphore_signal(barrier, inc=1, device_id=peer, device_id_type=MESH)

    for which, ref in enumerate((k_ref, v_ref)):
        wide[...] = ref[...].astype(jnp.float32)
        for h in range(8):
            snd[h, which * PIECE:(which + 1) * PIECE, :] = wide[pl.ds(h, PIECE, stride=8), :].astype(jnp.bfloat16)

    ids = id_ref[...].astype(jnp.float32)
    first = ids[:, :D]
    second = jnp.concatenate([ids[:, D:], jnp.zeros((1, 2 * D - ROWS), jnp.float32)], axis=1)
    tile = jnp.concatenate([first, second, jnp.zeros((14, D), jnp.float32)], axis=0)
    block = 2 * zh + c
    kv[col, block, HALF:, :] = tile.astype(jnp.bfloat16)

    pl.semaphore_wait(barrier, len(peers))

    spot = pl.ds(pl.multiple_of(2 * PIECE * g, 16), 2 * PIECE)

    for o in others:
        dz, dc, dg = o
        head = 2 * ((g + dg) % 4) + (c + dc) % 2
        pltpu.make_async_remote_copy(
            src_ref=snd.at[head], dst_ref=kv.at[col, block, spot],
            send_sem=zsend.at[dz], recv_sem=zrecv.at[block],
            device_id=inside(*o), device_id_type=MESH).start()
        if dg == 0:
            pltpu.make_async_remote_copy(
                src_ref=kv.at[col, block, pl.ds(HALF, 16)], dst_ref=kv.at[col, block, pl.ds(HALF, 16)],
                send_sem=zsend.at[dz], recv_sem=zrecv.at[block],
                device_id=inside(*o), device_id_type=MESH).start()
    pltpu.make_async_copy(snd.at[2 * g + c], kv.at[col, block, spot], lsem.at[0]).start()

    def wait_rows(sem, n):
        pltpu.make_async_copy(feat.at[pl.ds(0, n)], feat.at[pl.ds(0, n)], sem).wait()

    turned = jnp.transpose(tile[:8])
    lanes = lax.broadcasted_iota(jnp.int32, (D, D), 1).astype(jnp.float32)
    for part, size in ((0, D), (1, ROWS - D)):
        hot = jnp.where(turned[:size, part:part + 1] == lanes[:size], 1.0, 0.0)
        hot = jnp.broadcast_to(hot[:, None, :], (size, GROUP, D)).reshape(size * GROUP, D)
        for which in range(2):
            qst[which, pl.ds(part * D * GROUP, size * GROUP), D:] = hot.astype(jnp.bfloat16)

    def split(t, carry):
        rows = q_ref[pl.ds(t * 16 * 16, 256), :].astype(jnp.float32).reshape(16, 16, D)
        for which in range(2):
            qst[which, pl.ds(t * 128, 128), :D] = (
                rows[:, 8 * which:8 * which + 8, :].reshape(128, D).astype(jnp.bfloat16))
        return carry

    lax.fori_loop(0, ROWS // 16, split, 0)
    base = pl.multiple_of(c * MC, MC)
    qcopy = pltpu.make_async_remote_copy(
        src_ref=qst.at[1 - c], dst_ref=qaug.at[pl.ds(base, MC)],
        send_sem=qsend, recv_sem=qrecv, device_id=sibling, device_id_type=MESH)
    qcopy.start()
    qlocal = pltpu.make_async_copy(qst.at[c], qaug.at[pl.ds(base, MC)], lsem.at[1])
    qlocal.start()
    ones[...] = jnp.ones_like(ones)

    def order(t):
        return 2 * ((zh + t // 2) % 2) + (c + t) % 2

    def hands(step, who, b, gox, gop, gom):
        for direction, (go, target) in enumerate(((gox, east), (gop, plus), (gom, minus))):
            @pl.when(go)
            def _(direction=direction, target=target):
                pltpu.make_async_remote_copy(
                    src_ref=kv.at[who, b], dst_ref=kv.at[who, b],
                    send_sem=ssem.at[step, direction], recv_sem=rsem.at[who, b],
                    device_id=target, device_id_type=MESH).start()

    def handed(step, who, gox, gop, gom):
        for direction, go in enumerate((gox, gop, gom)):
            @pl.when(go)
            def _(direction=direction):
                pltpu.make_async_copy(kv.at[who], kv.at[who], ssem.at[step, direction]).wait()

    own = (x < 3, y < 3, y == 0)

    def quarter(who, target, number):
        return pltpu.make_async_remote_copy(
            src_ref=kv.at[who, 3], dst_ref=kv.at[who, 3],
            send_sem=qtr.at[number], recv_sem=rsem.at[who, 3],
            device_id=target, device_id_type=MESH)

    def block_wait(sem):
        pltpu.make_async_copy(kv.at[0, 0], kv.at[0, 0], sem).wait()

    def features(i, who, b, near):
        flip = jnp.transpose(kv[who, b, HALF:, :].astype(jnp.float32)[:8])
        for p, size in ((0, D), (1, ROWS - D)):
            feat[pl.ds(i * ROWS + p * D, size), :] = jnp.where(
                flip[:size, p:p + 1] == lanes[:size], near, -FAR).astype(jnp.bfloat16)

    def scores(r0, keys):
        return lax.dot_general(qaug[pl.ds(r0, SUB), :], keys, (((1,), (1,)), ((), ())),
                               preferred_element_type=jnp.float32)

    def finish(r0, sc, vals, start):
        here = pl.ds(r0, SUB)
        n = sc.shape[1]
        peak = jnp.broadcast_to(jnp.max(sc, axis=1, keepdims=True) * SCALE, (SUB, D))
        if not start:
            old = top[here, :]
            peak = jnp.maximum(old, peak)
        parts = []
        for j in range(0, n, D):
            w = min(D, n - j)
            parts.append(jnp.exp2(sc[:, j:j + w] * SCALE - peak[:, :w]).astype(jnp.bfloat16))
        weights = jnp.concatenate(parts, axis=1)
        out = jnp.dot(weights, vals, preferred_element_type=jnp.float32)
        if start:
            acc[here, :] = out
        else:
            factor = jnp.exp2(old - peak)
            acc[here, :D] = acc[here, :D] * factor + out[:, :D]
            acc[here, D:] = acc[here, D:] * factor + out[:, D:]
        top[here, :] = peak

    def attend(r, blocks, start, unroll):
        n = len(blocks) * ROWS

        def keys():
            k = jnp.concatenate([kv[who, b, r0:r0 + PIECE, :] for who, b in blocks
                                 for r0 in range(0, HALF, 2 * PIECE)], axis=0)
            return jnp.concatenate([k, feat[:n, :]], axis=1)

        def vals():
            v = jnp.concatenate([kv[who, b, r0:r0 + PIECE, :] for who, b in blocks
                                 for r0 in range(PIECE, HALF, 2 * PIECE)], axis=0)
            return jnp.concatenate([v, ones[:n, :]], axis=1)

        sc = scores(r, keys())
        for u in range(unroll):
            here = r + u * SUB
            nxt = scores(here + SUB, keys()) if u + 1 < unroll else None
            if start:
                shape = (SUB, n)
                row = here + lax.broadcasted_iota(jnp.int32, shape, 0)
                when = lax.broadcasted_iota(jnp.int32, shape, 1)
                sc = jnp.where(when * GROUP <= row, sc, -FAR)
            finish(here, sc, vals(), start)
            sc = nxt

    def mark(blocks, nears):
        for i, ((who, b), near) in enumerate(zip(blocks, nears)):
            features(i, who, b, near)

    def sweep(blocks, nears, start, count, unroll):
        mark(blocks, nears)

        def body(t, carry):
            attend(pl.multiple_of(t * (SUB * unroll), SUB * unroll), blocks, start, unroll)
            return carry

        lax.fori_loop(0, count // (SUB * unroll), body, 0)

    wait_rows(lsem.at[0], 2 * PIECE)
    wait_rows(zrecv.at[block], 6 * PIECE)
    hands(0, col, block, *own)
    block_wait(zrecv.at[order(1)])
    hands(0, col, order(1), *own)
    qlocal.wait()
    qcopy.wait_recv()
    sweep([(col, 2 * zh), (col, 2 * zh + 1)], [0.0] * 2, True, M, 4)

    orders = by_lane(PLANES, y)
    back_w, lane_w, gox_w, gop_w, gom_w = by_lane((BACK, LANE, GOX, GOP, GOM), y)

    def step_of(k):
        back = pick(back_w, k)
        who = (x - back) * 4 + pick(lane_w, k)
        there = x >= back
        gox = there & (pick(gox_w, k) > 0) & (x < 3)
        gop = there & (pick(gop_w, k) > 0)
        gom = there & (pick(gom_w, k) > 0)
        lone = there & (zh == 0) & (back == 2) & (who % 4 == y) & ((y < 3) | (x == 2))
        return who, there, gox, gop, gom, lone

    def onward(k, t):
        who, there, gox, gop, gom, lone = step_of(k)
        b = order(t)

        @pl.when(gox | gop | gom | lone)
        def _():
            block_wait(rsem.at[who, b])
            hands(k + 1, who, b, gox, gop, gom)

            @pl.when(lone & (b == 3) & (y == 3))
            def _():
                quarter(who, east, 0).start()

    corner = (zh == 0) & (x == 3)

    def pairs_of(op):
        blocks, nears, present = [], [], []
        for pair in ((op % 256) // 16, op % 16):
            who, there, gox, gop, gom, lone = step_of(pair // 2)
            pairs = [order(2 * (pair % 2) + j) for j in range(2)]

            @pl.when(there & jnp.logical_not(gox | gop | gom | lone))
            def _(who=who, pairs=pairs):
                for b in pairs:
                    block_wait(rsem.at[who, b])

            blocks += [(jnp.where(there, who, col), b) for b in pairs]
            nears += [jnp.where(there, 0.0, -FAR)] * 2
            present.append(there)
        return blocks, nears, present[0] | present[1]

    def turn(i, carry):
        op = fetch(orders, i)

        @pl.when(op < 32)
        def _():
            onward(op // 4, op % 4)

        @pl.when((op >= 32) & (op < 64))
        def _():
            b = order(op % 4)
            block_wait(zrecv.at[b])
            hands(0, col, b, *own)

        @pl.when((op == 64) & (zh == 1))
        def _():
            sweep([(col, 0), (col, 1)], [0.0] * 2, False, M, 4)

        @pl.when(op >= 256)
        def _():
            blocks, nears, present = pairs_of(op)

            @pl.when(present)
            def _():
                sweep(blocks, nears, False, M, 4)

        @pl.when((i == LATE) & (zh == 0) & (x >= 2) & (y < 3))
        def _():
            quarter(col - 8, plus, 0).start()

        @pl.when((i == RELAY) & corner & (y == 3))
        def _():
            block_wait(rsem.at[3, 3])
            quarter(3, plus, 1).start()

        return carry

    last = len(ORDER[0]) - 1
    lax.fori_loop(0, last, turn, 0)

    @pl.when(((zh == 0) & (x >= 2) & (y >= 1)) | (corner & (y == 0)))
    def _():
        who = col - 9
        block_wait(rsem.at[who, 3])
        sweep([(who, 3)], [0.0], False, MC, 2)

    def result(b, ref, slot):
        def body(t, carry):
            here = pl.ds(pl.multiple_of(b * MC + t * 256, 256), 256)
            ref[slot, pl.ds(t * 256, 256), :] = (acc[here, :D] / acc[here, D:]).astype(jnp.bfloat16)
            return carry

        lax.fori_loop(0, MC // 256, body, 0)

    ocopy = pltpu.make_async_remote_copy(
        src_ref=obuf.at[0], dst_ref=o_ref.at[c],
        send_sem=osend, recv_sem=orecv, device_id=sibling, device_id_type=MESH)
    blocks, nears, present = pairs_of(fetch(orders, last))
    mark(blocks, nears)

    def final(h, carry):
        b = (1 - c + h) % 2

        @pl.when(present)
        def _():
            attend(pl.multiple_of(b * MC, MC), blocks, False, MC // SUB)

        @pl.when(h == 0)
        def _():
            result(b, obuf, 0)
            ocopy.start()

        @pl.when(h == 1)
        def _():
            result(b, o_ref, c)

        return carry

    lax.fori_loop(0, 2, final, 0)
    ocopy.wait_recv()

    ocopy.wait_send()
    qcopy.wait_send()
    wait_rows(zsend.at[0], 14 * PIECE + 16)
    pltpu.make_async_copy(kv.at[0, pl.ds(0, 2)], kv.at[0, pl.ds(0, 2)], zsend.at[1]).wait()
    handed(0, col, *own)

    for lane in range(4):
        @pl.when(y == lane)
        def _(lane=lane):
            for k, (back, _, gox, gop, gom) in enumerate(PLAN[lane]):
                if gox or gop or gom:
                    @pl.when(x >= back)
                    def _(k=k, go=(gox, gop, gom)):
                        for direction in range(3):
                            if go[direction]:
                                @pl.when((x < 3) | (direction > 0))
                                def _(direction=direction):
                                    pltpu.make_async_copy(kv.at[0], kv.at[0], ssem.at[k + 1, direction]).wait()

    @pl.when((zh == 0) & ((x == 2) | ((x == 3) & (y < 3))))
    def _():
        block_wait(qtr.at[0])

    @pl.when(corner & (y == 3))
    def _():
        block_wait(qtr.at[1])


def per_device(queries, keys, values, doc_ids):
    bf, f32 = jnp.bfloat16, jnp.float32
    dma = pltpu.SemaphoreType.DMA
    vmem = pl.BlockSpec(memory_space=pltpu.VMEM)
    out = pl.pallas_call(
        kernel,
        out_shape=jax.ShapeDtypeStruct((2, MC, D), bf),
        in_specs=[vmem] * 4,
        out_specs=vmem,
        scratch_shapes=[
            pltpu.VMEM((8 * PIECE, D), f32),
            pltpu.VMEM((8, 2 * PIECE, D), bf),
            pltpu.VMEM((16, 4, CHUNK, D), bf),
            pltpu.VMEM((2, MC, 2 * D), bf),
            pltpu.VMEM((M, 2 * D), bf),
            pltpu.VMEM((KEYS, D), bf),
            pltpu.VMEM((KEYS, D), bf),
            pltpu.VMEM((M, D), f32),
            pltpu.VMEM((M, 2 * D), f32),
            pltpu.VMEM((1, MC, D), bf),
            dma((2,)), dma((4,)), dma((2,)), dma, dma, dma, dma,
            dma((STEPS + 1, 3)), dma((16, 4)), dma((2,)),
        ],
        compiler_params=pltpu.CompilerParams(
            collective_id=0, has_side_effects=True, vmem_limit_bytes=56 * 1024 * 1024),
    )(queries.reshape(ROWS * 16, D), keys.reshape(8 * PIECE, D), values.reshape(8 * PIECE, D),
      doc_ids.reshape(1, ROWS))
    return jnp.swapaxes(out.reshape(2, ROWS, GROUP, D), 0, 1).reshape(ROWS, 2 * GROUP, D)


def solution(mesh):
    return jax.shard_map(
        per_device,
        mesh=mesh,
        in_specs=(
            P("seq", "head", None),
            P(("seq", "head"), None, None),
            P(("seq", "head"), None, None),
            P("seq"),
        ),
        out_specs=P("seq", "head", None),
        check_vma=False,
    )
```

```python
import functools
import math

import jax
import jax.numpy as jnp
from jax import lax
from jax.experimental import pallas as pl
from jax.experimental.pallas import tpu as pltpu
from jax.sharding import PartitionSpec as P

MESH = pl.DeviceIdType.MESH

ROWS = 192
PIECE = 48
GROUP = 8
D = 128
HALF = 2 * ROWS
CHUNK = HALF + 16
KEYS = 2 * HALF
M = 2 * ROWS * GROUP
MC = ROWS * GROUP
SUB = 768
FAR = 2.0**20
SCALE = (1.0 / math.sqrt(D)) * math.log2(math.e)

PLAN = (
    ((1, 0, 3, 1, 3), (1, 1, 2, 0, 1), (1, 3, 2, 3, 0), (2, 0, 0, 0, 0), (1, 2, 0, 0, 0), (2, 1, 0, 0, 0), (2, 3, 0, 0, 0), (2, 2, 0, 0, 0)),
    ((0, 0, 2, 3, 0), (1, 1, 3, 1, 3), (1, 0, 0, 0, 0), (1, 2, 2, 0, 0), (2, 1, 0, 0, 1), (1, 3, 0, 0, 0), (2, 2, 0, 0, 3), (2, 3, 0, 0, 0)),
    ((0, 1, 2, 3, 0), (1, 2, 3, 1, 3), (0, 0, 2, 0, 0), (1, 1, 0, 0, 0), (1, 3, 0, 0, 0), (2, 2, 0, 0, 1), (1, 0, 0, 0, 0), (2, 3, 0, 0, 3)),
    ((0, 2, 2, 0, 0), (0, 0, 0, 0, 0), (1, 3, 3, 3, 3), (0, 1, 2, 0, 0), (1, 2, 0, 3, 0), (1, 0, 0, 0, 1), (2, 3, 0, 1, 3), (1, 1, 0, 0, 0)),
)
STEPS = len(PLAN[0])
RELAY = 23
LATE = 22

ORDER = (
    (0, 1, 34, 8, 4, 35, 64, 9, 260, 5, 2, 12, 13, 354, 3, 282, 6, 14, 15, 455, 10, 7, 312, 11, 485, 445, 65, 505),
    (0, 4, 1, 5, 34, 258, 16, 35, 64, 17, 326, 2, 6, 24, 7, 387, 25, 3, 18, 449, 15, 425, 27, 373, 26, 478, 65, 447),
    (0, 4, 1, 5, 34, 258, 20, 35, 64, 21, 394, 6, 326, 7, 28, 2, 22, 316, 3, 29, 283, 487, 11, 30, 405, 31, 65, 509),
    (8, 9, 34, 258, 20, 24, 35, 16, 64, 21, 25, 330, 10, 454, 17, 11, 26, 389, 3, 27, 305, 18, 22, 478, 19, 15, 441, 383),
)


def packed(field):
    return [sum(step[field] << (2 * k) for k, step in enumerate(lane)) for lane in PLAN]


BACK, LANE, GOX, GOP, GOM = (packed(f) for f in range(5))


def by_lane(tables, y):
    words = []
    for table in tables:
        word = jnp.int32(table[3])
        for lane in range(3):
            word = jnp.where(y == lane, jnp.int32(table[lane]), word)
        words.append(word)
    return words


def pick(word, k):
    return lax.shift_right_logical(word, 2 * k) & 3


def plane(bit):
    words = [sum(((op >> bit) & 1) << i for i, op in enumerate(lane)) for lane in ORDER]
    return [w - (1 << 32) if w >= 1 << 31 else w for w in words]


PLANES = [plane(bit) for bit in range(9)]


def fetch(words, i):
    value = 0
    for bit, word in enumerate(words):
        value = value + (lax.shift_right_logical(word, i) & 1) * (1 << bit)
    return value


def kernel(q_hbm, k_ref, v_ref, id_ref, o_ref,
           q_ref, wide, snd, kv, qst, qaug, feat, ones, top, acc, obuf,
           zsend, zrecv, lsem, qsend, qrecv, osend, orecv, ssem, rsem, qtr):
    s = lax.axis_index("seq")
    g = lax.axis_index("head")
    x, y, zh, c = s // 16, (s // 4) % 4, (s // 2) % 2, s % 2
    col = s // 4
    low = s % 4

    def at(xx, yy):
        return ((xx * 4 + yy) * 4 + low, g)

    def inside(dz, dc, dg):
        return (col * 4 + ((zh + dz) % 2) * 2 + (c + dc) % 2, (g + dg) % 4)

    sibling = inside(0, 1, 0)
    east = at((x + 1) % 4, y)
    plus = at(x, (y + 1) % 4)
    minus = at(x, (y + 3) % 4)
    others = [(dz, dc, dg) for dz in (0, 1) for dc in (0, 1) for dg in (2, 1, 3, 0) if dz or dc or dg]

    load = pltpu.make_async_copy(q_hbm, q_ref, lsem.at[2])
    load.start()

    barrier = pltpu.get_barrier_semaphore()
    peers = [inside(*o) for o in others] + [east, at((x + 3) % 4, y), plus, minus]
    for peer in peers:
        pl.semaphore_signal(barrier, inc=1, device_id=peer, device_id_type=MESH)

    for which, ref in enumerate((k_ref, v_ref)):
        wide[...] = ref[...].astype(jnp.float32)
        for h in range(8):
            snd[h, which * PIECE:(which + 1) * PIECE, :] = wide[pl.ds(h, PIECE, stride=8), :].astype(jnp.bfloat16)

    ids = id_ref[...].astype(jnp.float32)
    first = ids[:, :D]
    second = jnp.concatenate([ids[:, D:], jnp.zeros((1, 2 * D - ROWS), jnp.float32)], axis=1)
    tile = jnp.concatenate([first, second, jnp.zeros((14, D), jnp.float32)], axis=0)
    block = 2 * zh + c
    kv[col, block, HALF:, :] = tile.astype(jnp.bfloat16)

    pl.semaphore_wait(barrier, len(peers))

    spot = pl.ds(pl.multiple_of(2 * PIECE * g, 16), 2 * PIECE)

    def spread(plane):
        for o in others:
            dz, dc, dg = o
            if dz != plane:
                continue
            head = 2 * ((g + dg) % 4) + (c + dc) % 2
            pltpu.make_async_remote_copy(
                src_ref=snd.at[head], dst_ref=kv.at[col, block, spot],
                send_sem=zsend.at[dz], recv_sem=zrecv.at[block],
                device_id=inside(*o), device_id_type=MESH).start()
            if dg == 0:
                pltpu.make_async_remote_copy(
                    src_ref=kv.at[col, block, pl.ds(HALF, 16)], dst_ref=kv.at[col, block, pl.ds(HALF, 16)],
                    send_sem=zsend.at[dz], recv_sem=zrecv.at[block],
                    device_id=inside(*o), device_id_type=MESH).start()

    spread(0)
    pltpu.make_async_copy(snd.at[2 * g + c], kv.at[col, block, spot], lsem.at[0]).start()

    def wait_rows(sem, n):
        pltpu.make_async_copy(feat.at[pl.ds(0, n)], feat.at[pl.ds(0, n)], sem).wait()

    turned = jnp.transpose(tile[:8])
    lanes = lax.broadcasted_iota(jnp.int32, (D, D), 1).astype(jnp.float32)
    for part, size in ((0, D), (1, ROWS - D)):
        hot = jnp.where(turned[:size, part:part + 1] == lanes[:size], 1.0, 0.0)
        hot = jnp.broadcast_to(hot[:, None, :], (size, GROUP, D)).reshape(size * GROUP, D)
        for which in range(2):
            qst[which, pl.ds(part * D * GROUP, size * GROUP), D:] = hot.astype(jnp.bfloat16)

    def split(t, carry):
        rows = q_ref[pl.ds(t * 16 * 16, 256), :].astype(jnp.float32).reshape(16, 16, D)
        for which in range(2):
            qst[which, pl.ds(t * 128, 128), :D] = (
                rows[:, 8 * which:8 * which + 8, :].reshape(128, D).astype(jnp.bfloat16))
        return carry

    load.wait()
    lax.fori_loop(0, ROWS // 16, split, 0)
    base = pl.multiple_of(c * MC, MC)
    qcopy = pltpu.make_async_remote_copy(
        src_ref=qst.at[1 - c], dst_ref=qaug.at[pl.ds(base, MC)],
        send_sem=qsend, recv_sem=qrecv, device_id=sibling, device_id_type=MESH)
    qcopy.start()
    qlocal = pltpu.make_async_copy(qst.at[c], qaug.at[pl.ds(base, MC)], lsem.at[1])
    qlocal.start()
    ones[...] = jnp.ones_like(ones)
    wait_rows(zsend.at[0], 14 * PIECE + 16)
    spread(1)

    def order(t):
        return 2 * ((zh + t // 2) % 2) + (c + t) % 2

    def hands(step, who, b, gox, gop, gom):
        for direction, (go, target) in enumerate(((gox, east), (gop, plus), (gom, minus))):
            @pl.when(go)
            def _(direction=direction, target=target):
                pltpu.make_async_remote_copy(
                    src_ref=kv.at[who, b], dst_ref=kv.at[who, b],
                    send_sem=ssem.at[step, direction], recv_sem=rsem.at[who, b],
                    device_id=target, device_id_type=MESH).start()

    def handed(step, who, gox, gop, gom):
        for direction, go in enumerate((gox, gop, gom)):
            @pl.when(go)
            def _(direction=direction):
                pltpu.make_async_copy(kv.at[who], kv.at[who], ssem.at[step, direction]).wait()

    own = (x < 3, y < 3, y == 0)

    def quarter(who, target, number):
        return pltpu.make_async_remote_copy(
            src_ref=kv.at[who, 3], dst_ref=kv.at[who, 3],
            send_sem=qtr.at[number], recv_sem=rsem.at[who, 3],
            device_id=target, device_id_type=MESH)

    def block_wait(sem):
        pltpu.make_async_copy(kv.at[0, 0], kv.at[0, 0], sem).wait()

    def features(i, who, b, near):
        flip = jnp.transpose(kv[who, b, HALF:, :].astype(jnp.float32)[:8])
        for p, size in ((0, D), (1, ROWS - D)):
            feat[pl.ds(i * ROWS + p * D, size), :] = jnp.where(
                flip[:size, p:p + 1] == lanes[:size], near, -FAR).astype(jnp.bfloat16)

    def scores(r0, keys):
        return lax.dot_general(qaug[pl.ds(r0, SUB), :], keys, (((1,), (1,)), ((), ())),
                               preferred_element_type=jnp.float32)

    def finish(r0, sc, vals, start):
        here = pl.ds(r0, SUB)
        n = sc.shape[1]
        peak = jnp.broadcast_to(jnp.max(sc, axis=1, keepdims=True) * SCALE, (SUB, D))
        if not start:
            old = top[here, :]
            peak = jnp.maximum(old, peak)
        parts = []
        for j in range(0, n, D):
            w = min(D, n - j)
            parts.append(jnp.exp2(sc[:, j:j + w] * SCALE - peak[:, :w]).astype(jnp.bfloat16))
        weights = jnp.concatenate(parts, axis=1)
        out = jnp.dot(weights, vals, preferred_element_type=jnp.float32)
        if start:
            acc[here, :] = out
        else:
            factor = jnp.exp2(old - peak)
            acc[here, :D] = acc[here, :D] * factor + out[:, :D]
            acc[here, D:] = acc[here, D:] * factor + out[:, D:]
        top[here, :] = peak

    def attend(r, blocks, start, unroll):
        n = len(blocks) * ROWS

        def keys():
            k = jnp.concatenate([kv[who, b, r0:r0 + PIECE, :] for who, b in blocks
                                 for r0 in range(0, HALF, 2 * PIECE)], axis=0)
            return jnp.concatenate([k, feat[:n, :]], axis=1)

        def vals():
            v = jnp.concatenate([kv[who, b, r0:r0 + PIECE, :] for who, b in blocks
                                 for r0 in range(PIECE, HALF, 2 * PIECE)], axis=0)
            return jnp.concatenate([v, ones[:n, :]], axis=1)

        sc = scores(r, keys())
        for u in range(unroll):
            here = r + u * SUB
            nxt = scores(here + SUB, keys()) if u + 1 < unroll else None
            if start:
                shape = (SUB, n)
                row = here + lax.broadcasted_iota(jnp.int32, shape, 0)
                when = lax.broadcasted_iota(jnp.int32, shape, 1)
                sc = jnp.where(when * GROUP <= row, sc, -FAR)
            finish(here, sc, vals(), start)
            sc = nxt

    def mark(blocks, nears):
        for i, ((who, b), near) in enumerate(zip(blocks, nears)):
            features(i, who, b, near)

    def sweep(blocks, nears, start, count, unroll):
        mark(blocks, nears)

        def body(t, carry):
            attend(pl.multiple_of(t * (SUB * unroll), SUB * unroll), blocks, start, unroll)
            return carry

        lax.fori_loop(0, count // (SUB * unroll), body, 0)

    wait_rows(lsem.at[0], 2 * PIECE)
    wait_rows(zrecv.at[block], 6 * PIECE)
    hands(0, col, block, *own)
    block_wait(zrecv.at[order(1)])
    hands(0, col, order(1), *own)
    qlocal.wait()
    qcopy.wait_recv()
    sweep([(col, 2 * zh), (col, 2 * zh + 1)], [0.0] * 2, True, M, 4)

    orders = by_lane(PLANES, y)
    back_w, lane_w, gox_w, gop_w, gom_w = by_lane((BACK, LANE, GOX, GOP, GOM), y)

    def step_of(k, t):
        bit = jnp.where(t == 3, 2, 1)
        back = pick(back_w, k)
        who = (x - back) * 4 + pick(lane_w, k)
        there = x >= back
        gox = there & ((pick(gox_w, k) & bit) > 0) & (x < 3)
        gop = there & ((pick(gop_w, k) & bit) > 0)
        gom = there & ((pick(gom_w, k) & bit) > 0)
        lone = (zh == 0) & (x == 2) & (y == 3) & (who == 3)
        return who, there, gox, gop, gom, lone

    def onward(k, t):
        who, there, gox, gop, gom, lone = step_of(k, t)
        b = order(t)

        @pl.when(gox | gop | gom)
        def _():
            block_wait(rsem.at[who, b])
            hands(k + 1, who, b, gox, gop, gom)

            @pl.when(lone & (b == 3))
            def _():
                quarter(who, east, 0).start()

    corner = (zh == 0) & (x == 3)

    def pairs_of(op):
        blocks, nears, present = [], [], []
        for pair in ((op % 256) // 16, op % 16):
            pairs = []
            for j in range(2):
                t = 2 * (pair % 2) + j
                who, there, gox, gop, gom, lone = step_of(pair // 2, t)
                b = order(t)
                pairs.append(b)

                @pl.when(there & jnp.logical_not(gox | gop | gom))
                def _(who=who, b=b):
                    block_wait(rsem.at[who, b])

            blocks += [(jnp.where(there, who, col), b) for b in pairs]
            nears += [jnp.where(there, 0.0, -FAR)] * 2
            present.append(there)
        return blocks, nears, present[0] | present[1]

    def turn(i, carry):
        op = fetch(orders, i)

        @pl.when(op < 32)
        def _():
            onward(op // 4, op % 4)

        @pl.when((op >= 32) & (op < 64))
        def _():
            b = order(op % 4)
            block_wait(zrecv.at[b])
            hands(0, col, b, *own)

        @pl.when((op == 64) & (zh == 1))
        def _():
            sweep([(col, 0), (col, 1)], [0.0] * 2, False, M, 4)

        @pl.when(op >= 256)
        def _():
            blocks, nears, present = pairs_of(op)

            @pl.when(present)
            def _():
                sweep(blocks, nears, False, M, 4)

        @pl.when((i == LATE) & (zh == 0) & (x >= 2) & (y < 3))
        def _():
            quarter(col - 8, plus, 0).start()

        @pl.when((i == RELAY) & corner & (y == 3))
        def _():
            block_wait(rsem.at[3, 3])
            quarter(3, plus, 1).start()

        return carry

    last = len(ORDER[0]) - 1
    lax.fori_loop(0, last, turn, 0)

    @pl.when(((zh == 0) & (x >= 2) & (y >= 1)) | (corner & (y == 0)))
    def _():
        who = col - 9
        block_wait(rsem.at[who, 3])
        sweep([(who, 3)], [0.0], False, MC, 2)

    def result(b, ref, slot):
        def body(t, carry):
            here = pl.ds(pl.multiple_of(b * MC + t * 256, 256), 256)
            ref[slot, pl.ds(t * 256, 256), :] = (acc[here, :D] / acc[here, D:]).astype(jnp.bfloat16)
            return carry

        lax.fori_loop(0, MC // 256, body, 0)

    ocopy = pltpu.make_async_remote_copy(
        src_ref=obuf.at[0], dst_ref=o_ref.at[c],
        send_sem=osend, recv_sem=orecv, device_id=sibling, device_id_type=MESH)
    blocks, nears, present = pairs_of(fetch(orders, last))
    mark(blocks, nears)

    def final(h, carry):
        b = (1 - c + h) % 2

        @pl.when(present)
        def _():
            attend(pl.multiple_of(b * MC, MC), blocks, False, MC // SUB)

        @pl.when(h == 0)
        def _():
            result(b, obuf, 0)
            ocopy.start()

        @pl.when(h == 1)
        def _():
            result(b, o_ref, c)

        return carry

    lax.fori_loop(0, 2, final, 0)
    ocopy.wait_recv()

    ocopy.wait_send()
    qcopy.wait_send()
    pltpu.make_async_copy(kv.at[0, pl.ds(0, 2)], kv.at[0, pl.ds(0, 2)], zsend.at[1]).wait()
    handed(0, col, *own)

    for lane in range(4):
        @pl.when(y == lane)
        def _(lane=lane):
            for k, (back, _, gox, gop, gom) in enumerate(PLAN[lane]):
                if gox or gop or gom:
                    @pl.when(x >= back)
                    def _(k=k, go=(gox, gop, gom)):
                        for direction in range(3):
                            if go[direction]:
                                @pl.when((x < 3) | (direction > 0))
                                def _(direction=direction):
                                    some = kv.at[0, pl.ds(0, (0, 3, 1, 4)[go[direction]])]
                                    pltpu.make_async_copy(some, some, ssem.at[k + 1, direction]).wait()

    @pl.when((zh == 0) & ((x == 2) | ((x == 3) & (y < 3))))
    def _():
        block_wait(qtr.at[0])

    @pl.when(corner & (y == 3))
    def _():
        block_wait(qtr.at[1])


def per_device(queries, keys, values, doc_ids):
    bf, f32 = jnp.bfloat16, jnp.float32
    dma = pltpu.SemaphoreType.DMA
    vmem = pl.BlockSpec(memory_space=pltpu.VMEM)
    out = pl.pallas_call(
        kernel,
        out_shape=jax.ShapeDtypeStruct((2, MC, D), bf),
        in_specs=[pl.BlockSpec(memory_space=pl.ANY)] + [vmem] * 3,
        out_specs=vmem,
        scratch_shapes=[
            pltpu.VMEM((ROWS * 16, D), bf),
            pltpu.VMEM((8 * PIECE, D), f32),
            pltpu.VMEM((8, 2 * PIECE, D), bf),
            pltpu.VMEM((16, 4, CHUNK, D), bf),
            pltpu.VMEM((2, MC, 2 * D), bf),
            pltpu.VMEM((M, 2 * D), bf),
            pltpu.VMEM((KEYS, D), bf),
            pltpu.VMEM((KEYS, D), bf),
            pltpu.VMEM((M, D), f32),
            pltpu.VMEM((M, 2 * D), f32),
            pltpu.VMEM((1, MC, D), bf),
            dma((2,)), dma((4,)), dma((3,)), dma, dma, dma, dma,
            dma((STEPS + 1, 3)), dma((16, 4)), dma((2,)),
        ],
        compiler_params=pltpu.CompilerParams(
            collective_id=0, has_side_effects=True, vmem_limit_bytes=56 * 1024 * 1024),
    )(queries.reshape(ROWS * 16, D), keys.reshape(8 * PIECE, D), values.reshape(8 * PIECE, D),
      doc_ids.reshape(1, ROWS))
    return jnp.swapaxes(out.reshape(2, ROWS, GROUP, D), 0, 1).reshape(ROWS, 2 * GROUP, D)


def solution(mesh):
    return jax.shard_map(
        per_device,
        mesh=mesh,
        in_specs=(
            P("seq", "head", None),
            P(("seq", "head"), None, None),
            P(("seq", "head"), None, None),
            P("seq"),
        ),
        out_specs=P("seq", "head", None),
        check_vma=False,
    )
```

```python
import functools
import math

import jax
import jax.numpy as jnp
from jax import lax
from jax.experimental import pallas as pl
from jax.experimental.pallas import tpu as pltpu
from jax.sharding import PartitionSpec as P

MESH = pl.DeviceIdType.MESH

ROWS = 192
PIECE = 48
GROUP = 8
D = 128
HALF = 2 * ROWS
CHUNK = HALF + 16
KEYS = 2 * HALF
M = 2 * ROWS * GROUP
MC = ROWS * GROUP
SUB = 768
FAR = 2.0**20
SCALE = (1.0 / math.sqrt(D)) * math.log2(math.e)

PLAN = (
    ((1, 0, 3, 1, 3), (1, 1, 2, 0, 1), (1, 3, 2, 3, 0), (2, 0, 0, 0, 0), (1, 2, 0, 0, 0), (2, 1, 0, 0, 0), (2, 3, 0, 0, 0), (2, 2, 0, 0, 0)),
    ((0, 0, 2, 3, 0), (1, 1, 3, 1, 3), (1, 0, 0, 0, 0), (1, 2, 2, 0, 0), (2, 1, 0, 0, 1), (1, 3, 0, 0, 0), (2, 2, 0, 0, 3), (2, 3, 0, 0, 0)),
    ((0, 1, 2, 3, 0), (1, 2, 3, 1, 3), (0, 0, 2, 0, 0), (1, 1, 0, 0, 0), (1, 3, 0, 0, 0), (2, 2, 0, 0, 1), (1, 0, 0, 0, 0), (2, 3, 0, 0, 3)),
    ((0, 2, 2, 0, 0), (0, 0, 0, 0, 0), (1, 3, 3, 3, 3), (0, 1, 2, 0, 0), (1, 2, 0, 3, 0), (1, 0, 0, 0, 1), (2, 3, 0, 1, 3), (1, 1, 0, 0, 0)),
)
STEPS = len(PLAN[0])
RELAY = 23
LATE = 22

ORDER = (
    (0, 1, 34, 8, 4, 35, 64, 9, 260, 5, 2, 12, 13, 354, 3, 282, 6, 14, 15, 455, 10, 7, 312, 11, 485, 445, 65, 505),
    (0, 4, 1, 5, 34, 258, 16, 35, 64, 17, 326, 2, 6, 24, 7, 387, 25, 3, 18, 449, 15, 425, 27, 373, 26, 478, 65, 447),
    (0, 4, 1, 5, 34, 258, 20, 35, 64, 21, 394, 6, 326, 7, 28, 2, 22, 316, 3, 29, 283, 487, 11, 30, 405, 31, 65, 509),
    (8, 9, 34, 258, 20, 24, 35, 16, 64, 21, 25, 330, 10, 454, 17, 11, 26, 389, 3, 27, 305, 18, 22, 478, 19, 15, 441, 383),
)


def packed(field):
    return [sum(step[field] << (2 * k) for k, step in enumerate(lane)) for lane in PLAN]


BACK, LANE, GOX, GOP, GOM = (packed(f) for f in range(5))


def by_lane(tables, y):
    words = []
    for table in tables:
        word = jnp.int32(table[3])
        for lane in range(3):
            word = jnp.where(y == lane, jnp.int32(table[lane]), word)
        words.append(word)
    return words


def pick(word, k):
    return lax.shift_right_logical(word, 2 * k) & 3


def plane(bit):
    words = [sum(((op >> bit) & 1) << i for i, op in enumerate(lane)) for lane in ORDER]
    return [w - (1 << 32) if w >= 1 << 31 else w for w in words]


PLANES = [plane(bit) for bit in range(9)]


def fetch(words, i):
    value = 0
    for bit, word in enumerate(words):
        value = value + (lax.shift_right_logical(word, i) & 1) * (1 << bit)
    return value


def kernel(q_hbm, k_ref, v_ref, id_ref, o_ref,
           q_ref, wide, snd, kv, qst, qaug, feat, ones, top, acc, obuf,
           zsend, zrecv, lsem, qsend, qrecv, osend, orecv, ssem, rsem, qtr):
    s = lax.axis_index("seq")
    g = lax.axis_index("head")
    x, y, zh, c = s // 16, (s // 4) % 4, (s // 2) % 2, s % 2
    col = s // 4
    low = s % 4

    def at(xx, yy):
        return ((xx * 4 + yy) * 4 + low, g)

    def inside(dz, dc, dg):
        return (col * 4 + ((zh + dz) % 2) * 2 + (c + dc) % 2, (g + dg) % 4)

    sibling = inside(0, 1, 0)
    east = at((x + 1) % 4, y)
    plus = at(x, (y + 1) % 4)
    minus = at(x, (y + 3) % 4)
    others = [(dz, dc, dg) for dz in (0, 1) for dc in (0, 1) for dg in (2, 1, 3, 0) if dz or dc or dg]

    load = pltpu.make_async_copy(q_hbm, q_ref, lsem.at[2])
    load.start()

    barrier = pltpu.get_barrier_semaphore()
    peers = [inside(*o) for o in others] + [east, at((x + 3) % 4, y), plus, minus]
    for peer in peers:
        pl.semaphore_signal(barrier, inc=1, device_id=peer, device_id_type=MESH)

    for which, ref in enumerate((k_ref, v_ref)):
        wide[...] = ref[...].astype(jnp.float32)
        for h in range(8):
            snd[h, which * PIECE:(which + 1) * PIECE, :] = wide[pl.ds(h, PIECE, stride=8), :].astype(jnp.bfloat16)

    ids = id_ref[...].astype(jnp.float32)
    first = ids[:, :D]
    second = jnp.concatenate([ids[:, D:], jnp.zeros((1, 2 * D - ROWS), jnp.float32)], axis=1)
    tile = jnp.concatenate([first, second, jnp.zeros((14, D), jnp.float32)], axis=0)
    block = 2 * zh + c
    kv[col, block, HALF:, :] = tile.astype(jnp.bfloat16)

    turned = jnp.transpose(tile[:8])
    lanes = lax.broadcasted_iota(jnp.int32, (D, D), 1).astype(jnp.float32)
    def queries():
        for part, size in ((0, D), (1, ROWS - D)):
            hot = jnp.where(turned[:size, part:part + 1] == lanes[:size], 1.0, 0.0)
            hot = jnp.broadcast_to(hot[:, None, :], (size, GROUP, D)).reshape(size * GROUP, D)
            for which in range(2):
                qst[which, pl.ds(part * D * GROUP, size * GROUP), D:] = hot.astype(jnp.bfloat16)

        def split(t, carry):
            rows = q_ref[pl.ds(t * 16 * 16, 256), :].astype(jnp.float32).reshape(16, 16, D)
            for which in range(2):
                qst[which, pl.ds(t * 128, 128), :D] = (
                    rows[:, 8 * which:8 * which + 8, :].reshape(128, D).astype(jnp.bfloat16))
            return carry

        load.wait()
        lax.fori_loop(0, ROWS // 16, split, 0)

    @pl.when(zh == 0)
    def _():
        queries()

    pl.semaphore_wait(barrier, len(peers))

    spot = pl.ds(pl.multiple_of(2 * PIECE * g, 16), 2 * PIECE)

    def spread(plane):
        for o in others:
            dz, dc, dg = o
            if dz != plane:
                continue
            head = 2 * ((g + dg) % 4) + (c + dc) % 2
            pltpu.make_async_remote_copy(
                src_ref=snd.at[head], dst_ref=kv.at[col, block, spot],
                send_sem=zsend.at[dz], recv_sem=zrecv.at[block],
                device_id=inside(*o), device_id_type=MESH).start()
            if dg == 0:
                pltpu.make_async_remote_copy(
                    src_ref=kv.at[col, block, pl.ds(HALF, 16)], dst_ref=kv.at[col, block, pl.ds(HALF, 16)],
                    send_sem=zsend.at[dz], recv_sem=zrecv.at[block],
                    device_id=inside(*o), device_id_type=MESH).start()

    spread(0)
    spread(1)
    pltpu.make_async_copy(snd.at[2 * g + c], kv.at[col, block, spot], lsem.at[0]).start()

    def wait_rows(sem, n):
        pltpu.make_async_copy(feat.at[pl.ds(0, n)], feat.at[pl.ds(0, n)], sem).wait()

    @pl.when(zh == 1)
    def _():
        queries()

    base = pl.multiple_of(c * MC, MC)
    qcopy = pltpu.make_async_remote_copy(
        src_ref=qst.at[1 - c], dst_ref=qaug.at[pl.ds(base, MC)],
        send_sem=qsend, recv_sem=qrecv, device_id=sibling, device_id_type=MESH)
    qcopy.start()
    qlocal = pltpu.make_async_copy(qst.at[c], qaug.at[pl.ds(base, MC)], lsem.at[1])
    qlocal.start()
    ones[...] = jnp.ones_like(ones)

    def order(t):
        return 2 * ((zh + t // 2) % 2) + (c + t) % 2

    def hands(step, who, b, gox, gop, gom):
        for direction, (go, target) in enumerate(((gox, east), (gop, plus), (gom, minus))):
            @pl.when(go)
            def _(direction=direction, target=target):
                pltpu.make_async_remote_copy(
                    src_ref=kv.at[who, b], dst_ref=kv.at[who, b],
                    send_sem=ssem.at[step, direction], recv_sem=rsem.at[who, b],
                    device_id=target, device_id_type=MESH).start()

    def handed(step, who, gox, gop, gom):
        for direction, go in enumerate((gox, gop, gom)):
            @pl.when(go)
            def _(direction=direction):
                pltpu.make_async_copy(kv.at[who], kv.at[who], ssem.at[step, direction]).wait()

    own = (x < 3, y < 3, y == 0)

    def quarter(who, target, number):
        return pltpu.make_async_remote_copy(
            src_ref=kv.at[who, 3], dst_ref=kv.at[who, 3],
            send_sem=qtr.at[number], recv_sem=rsem.at[who, 3],
            device_id=target, device_id_type=MESH)

    def block_wait(sem):
        pltpu.make_async_copy(kv.at[0, 0], kv.at[0, 0], sem).wait()

    def features(i, who, b, near):
        flip = jnp.transpose(kv[who, b, HALF:, :].astype(jnp.float32)[:8])
        for p, size in ((0, D), (1, ROWS - D)):
            feat[pl.ds(i * ROWS + p * D, size), :] = jnp.where(
                flip[:size, p:p + 1] == lanes[:size], near, -FAR).astype(jnp.bfloat16)

    def scores(r0, keys):
        return lax.dot_general(qaug[pl.ds(r0, SUB), :], keys, (((1,), (1,)), ((), ())),
                               preferred_element_type=jnp.float32)

    def finish(r0, sc, vals, start):
        here = pl.ds(r0, SUB)
        n = sc.shape[1]
        peak = jnp.broadcast_to(jnp.max(sc, axis=1, keepdims=True) * SCALE, (SUB, D))
        if not start:
            old = top[here, :]
            peak = jnp.maximum(old, peak)
        parts = []
        for j in range(0, n, D):
            w = min(D, n - j)
            parts.append(jnp.exp2(sc[:, j:j + w] * SCALE - peak[:, :w]).astype(jnp.bfloat16))
        weights = jnp.concatenate(parts, axis=1)
        out = jnp.dot(weights, vals, preferred_element_type=jnp.float32)
        if start:
            acc[here, :] = out
        else:
            factor = jnp.exp2(old - peak)
            acc[here, :D] = acc[here, :D] * factor + out[:, :D]
            acc[here, D:] = acc[here, D:] * factor + out[:, D:]
        top[here, :] = peak

    def attend(r, blocks, start, unroll):
        n = len(blocks) * ROWS

        def keys():
            k = jnp.concatenate([kv[who, b, r0:r0 + PIECE, :] for who, b in blocks
                                 for r0 in range(0, HALF, 2 * PIECE)], axis=0)
            return jnp.concatenate([k, feat[:n, :]], axis=1)

        def vals():
            v = jnp.concatenate([kv[who, b, r0:r0 + PIECE, :] for who, b in blocks
                                 for r0 in range(PIECE, HALF, 2 * PIECE)], axis=0)
            return jnp.concatenate([v, ones[:n, :]], axis=1)

        sc = scores(r, keys())
        for u in range(unroll):
            here = r + u * SUB
            nxt = scores(here + SUB, keys()) if u + 1 < unroll else None
            if start:
                shape = (SUB, n)
                row = here + lax.broadcasted_iota(jnp.int32, shape, 0)
                when = lax.broadcasted_iota(jnp.int32, shape, 1)
                sc = jnp.where(when * GROUP <= row, sc, -FAR)
            finish(here, sc, vals(), start)
            sc = nxt

    def mark(blocks, nears):
        for i, ((who, b), near) in enumerate(zip(blocks, nears)):
            features(i, who, b, near)

    def sweep(blocks, nears, start, count, unroll):
        mark(blocks, nears)

        def body(t, carry):
            attend(pl.multiple_of(t * (SUB * unroll), SUB * unroll), blocks, start, unroll)
            return carry

        lax.fori_loop(0, count // (SUB * unroll), body, 0)

    wait_rows(lsem.at[0], 2 * PIECE)
    wait_rows(zrecv.at[block], 6 * PIECE)
    hands(0, col, block, *own)
    block_wait(zrecv.at[order(1)])
    hands(0, col, order(1), *own)
    qlocal.wait()
    qcopy.wait_recv()
    sweep([(col, 2 * zh), (col, 2 * zh + 1)], [0.0] * 2, True, M, 4)

    orders = by_lane(PLANES, y)
    back_w, lane_w, gox_w, gop_w, gom_w = by_lane((BACK, LANE, GOX, GOP, GOM), y)

    def step_of(k, t):
        bit = jnp.where(t == 3, 2, 1)
        back = pick(back_w, k)
        who = (x - back) * 4 + pick(lane_w, k)
        there = x >= back
        gox = there & ((pick(gox_w, k) & bit) > 0) & (x < 3)
        gop = there & ((pick(gop_w, k) & bit) > 0)
        gom = there & ((pick(gom_w, k) & bit) > 0)
        lone = (zh == 0) & (x == 2) & (y == 3) & (who == 3)
        return who, there, gox, gop, gom, lone

    def onward(k, t):
        who, there, gox, gop, gom, lone = step_of(k, t)
        b = order(t)

        @pl.when(gox | gop | gom)
        def _():
            block_wait(rsem.at[who, b])
            hands(k + 1, who, b, gox, gop, gom)

            @pl.when(lone & (b == 3))
            def _():
                quarter(who, east, 0).start()

    corner = (zh == 0) & (x == 3)

    def pairs_of(op):
        blocks, nears, present = [], [], []
        for pair in ((op % 256) // 16, op % 16):
            pairs = []
            for j in range(2):
                t = 2 * (pair % 2) + j
                who, there, gox, gop, gom, lone = step_of(pair // 2, t)
                b = order(t)
                pairs.append(b)

                @pl.when(there & jnp.logical_not(gox | gop | gom))
                def _(who=who, b=b):
                    block_wait(rsem.at[who, b])

            blocks += [(jnp.where(there, who, col), b) for b in pairs]
            nears += [jnp.where(there, 0.0, -FAR)] * 2
            present.append(there)
        return blocks, nears, present[0] | present[1]

    def turn(i, carry):
        op = fetch(orders, i)

        @pl.when(op < 32)
        def _():
            onward(op // 4, op % 4)

        @pl.when((op >= 32) & (op < 64))
        def _():
            b = order(op % 4)
            block_wait(zrecv.at[b])
            hands(0, col, b, *own)

        @pl.when((op == 64) & (zh == 1))
        def _():
            sweep([(col, 0), (col, 1)], [0.0] * 2, False, M, 4)

        @pl.when(op >= 256)
        def _():
            blocks, nears, present = pairs_of(op)

            @pl.when(present)
            def _():
                sweep(blocks, nears, False, M, 4)

        @pl.when((i == LATE) & (zh == 0) & (x >= 2) & (y < 3))
        def _():
            quarter(col - 8, plus, 0).start()

        @pl.when((i == RELAY) & corner & (y == 3))
        def _():
            block_wait(rsem.at[3, 3])
            quarter(3, plus, 1).start()

        return carry

    last = len(ORDER[0]) - 1
    lax.fori_loop(0, last, turn, 0)

    @pl.when(((zh == 0) & (x >= 2) & (y >= 1)) | (corner & (y == 0)))
    def _():
        who = col - 9
        block_wait(rsem.at[who, 3])
        sweep([(who, 3)], [0.0], False, MC, 2)

    def result(b, ref, slot):
        def body(t, carry):
            here = pl.ds(pl.multiple_of(b * MC + t * 256, 256), 256)
            ref[slot, pl.ds(t * 256, 256), :] = (acc[here, :D] / acc[here, D:]).astype(jnp.bfloat16)
            return carry

        lax.fori_loop(0, MC // 256, body, 0)

    ocopy = pltpu.make_async_remote_copy(
        src_ref=obuf.at[0], dst_ref=o_ref.at[c],
        send_sem=osend, recv_sem=orecv, device_id=sibling, device_id_type=MESH)
    blocks, nears, present = pairs_of(fetch(orders, last))
    mark(blocks, nears)

    def final(h, carry):
        b = (1 - c + h) % 2

        @pl.when(present)
        def _():
            attend(pl.multiple_of(b * MC, MC), blocks, False, MC // SUB)

        @pl.when(h == 0)
        def _():
            result(b, obuf, 0)
            ocopy.start()

        @pl.when(h == 1)
        def _():
            result(b, o_ref, c)

        return carry

    lax.fori_loop(0, 2, final, 0)
    ocopy.wait_recv()

    ocopy.wait_send()
    qcopy.wait_send()
    wait_rows(zsend.at[0], 14 * PIECE + 16)
    pltpu.make_async_copy(kv.at[0, pl.ds(0, 2)], kv.at[0, pl.ds(0, 2)], zsend.at[1]).wait()
    handed(0, col, *own)

    for lane in range(4):
        @pl.when(y == lane)
        def _(lane=lane):
            for k, (back, _, gox, gop, gom) in enumerate(PLAN[lane]):
                if gox or gop or gom:
                    @pl.when(x >= back)
                    def _(k=k, go=(gox, gop, gom)):
                        for direction in range(3):
                            if go[direction]:
                                @pl.when((x < 3) | (direction > 0))
                                def _(direction=direction):
                                    some = kv.at[0, pl.ds(0, (0, 3, 1, 4)[go[direction]])]
                                    pltpu.make_async_copy(some, some, ssem.at[k + 1, direction]).wait()

    @pl.when((zh == 0) & ((x == 2) | ((x == 3) & (y < 3))))
    def _():
        block_wait(qtr.at[0])

    @pl.when(corner & (y == 3))
    def _():
        block_wait(qtr.at[1])


def per_device(queries, keys, values, doc_ids):
    bf, f32 = jnp.bfloat16, jnp.float32
    dma = pltpu.SemaphoreType.DMA
    vmem = pl.BlockSpec(memory_space=pltpu.VMEM)
    out = pl.pallas_call(
        kernel,
        out_shape=jax.ShapeDtypeStruct((2, MC, D), bf),
        in_specs=[pl.BlockSpec(memory_space=pl.ANY)] + [vmem] * 3,
        out_specs=vmem,
        scratch_shapes=[
            pltpu.VMEM((ROWS * 16, D), bf),
            pltpu.VMEM((8 * PIECE, D), f32),
            pltpu.VMEM((8, 2 * PIECE, D), bf),
            pltpu.VMEM((16, 4, CHUNK, D), bf),
            pltpu.VMEM((2, MC, 2 * D), bf),
            pltpu.VMEM((M, 2 * D), bf),
            pltpu.VMEM((KEYS, D), bf),
            pltpu.VMEM((KEYS, D), bf),
            pltpu.VMEM((M, D), f32),
            pltpu.VMEM((M, 2 * D), f32),
            pltpu.VMEM((1, MC, D), bf),
            dma((2,)), dma((4,)), dma((3,)), dma, dma, dma, dma,
            dma((STEPS + 1, 3)), dma((16, 4)), dma((2,)),
        ],
        compiler_params=pltpu.CompilerParams(
            collective_id=0, has_side_effects=True, vmem_limit_bytes=56 * 1024 * 1024),
    )(queries.reshape(ROWS * 16, D), keys.reshape(8 * PIECE, D), values.reshape(8 * PIECE, D),
      doc_ids.reshape(1, ROWS))
    return jnp.swapaxes(out.reshape(2, ROWS, GROUP, D), 0, 1).reshape(ROWS, 2 * GROUP, D)


def solution(mesh):
    return jax.shard_map(
        per_device,
        mesh=mesh,
        in_specs=(
            P("seq", "head", None),
            P(("seq", "head"), None, None),
            P(("seq", "head"), None, None),
            P("seq"),
        ),
        out_specs=P("seq", "head", None),
        check_vma=False,
    )
```

```python
import functools
import math

import jax
import jax.numpy as jnp
from jax import lax
from jax.experimental import pallas as pl
from jax.experimental.pallas import tpu as pltpu
from jax.sharding import PartitionSpec as P

MESH = pl.DeviceIdType.MESH

ROWS = 192
PIECE = 48
GROUP = 8
D = 128
HALF = 2 * ROWS
CHUNK = HALF + 16
KEYS = 2 * HALF
M = 2 * ROWS * GROUP
MC = ROWS * GROUP
SUB = 768
FAR = 2.0**20
SCALE = (1.0 / math.sqrt(D)) * math.log2(math.e)

PLAN = (
    ((1, 0, 3, 1, 3), (1, 1, 2, 0, 1), (1, 3, 2, 3, 0), (2, 0, 0, 0, 0), (1, 2, 0, 0, 0), (2, 1, 0, 0, 0), (2, 3, 0, 0, 0), (2, 2, 0, 0, 0)),
    ((0, 0, 2, 3, 0), (1, 1, 3, 1, 3), (1, 0, 0, 0, 0), (1, 2, 2, 0, 0), (2, 1, 0, 0, 1), (1, 3, 0, 0, 0), (2, 2, 0, 0, 3), (2, 3, 0, 0, 0)),
    ((0, 1, 2, 3, 0), (1, 2, 3, 1, 3), (0, 0, 2, 0, 0), (1, 1, 0, 0, 0), (1, 3, 0, 0, 0), (2, 2, 0, 0, 1), (1, 0, 0, 0, 0), (2, 3, 0, 0, 3)),
    ((0, 2, 2, 0, 0), (0, 0, 0, 0, 0), (1, 3, 3, 3, 3), (0, 1, 2, 0, 0), (1, 2, 0, 3, 0), (1, 0, 0, 0, 1), (2, 3, 0, 1, 3), (1, 1, 0, 0, 0)),
)
STEPS = len(PLAN[0])
RELAY = 23
LATE = 22

ORDER = (
    (0, 1, 34, 8, 4, 35, 64, 9, 260, 5, 2, 12, 13, 354, 3, 282, 6, 14, 15, 455, 10, 7, 312, 11, 485, 445, 65, 505),
    (0, 4, 1, 5, 34, 258, 16, 35, 64, 17, 326, 2, 6, 24, 7, 387, 25, 3, 18, 449, 15, 425, 27, 373, 26, 478, 65, 447),
    (0, 4, 1, 5, 34, 258, 20, 35, 64, 21, 394, 6, 326, 7, 28, 2, 22, 316, 3, 29, 283, 487, 11, 30, 405, 31, 65, 509),
    (8, 9, 34, 258, 20, 24, 35, 16, 64, 21, 25, 330, 10, 454, 17, 11, 26, 389, 3, 27, 305, 18, 22, 478, 19, 15, 441, 383),
)


def packed(field):
    return [sum(step[field] << (2 * k) for k, step in enumerate(lane)) for lane in PLAN]


BACK, LANE, GOX, GOP, GOM = (packed(f) for f in range(5))


def by_lane(tables, y):
    words = []
    for table in tables:
        word = jnp.int32(table[3])
        for lane in range(3):
            word = jnp.where(y == lane, jnp.int32(table[lane]), word)
        words.append(word)
    return words


def pick(word, k):
    return lax.shift_right_logical(word, 2 * k) & 3


def plane(bit):
    words = [sum(((op >> bit) & 1) << i for i, op in enumerate(lane)) for lane in ORDER]
    return [w - (1 << 32) if w >= 1 << 31 else w for w in words]


PLANES = [plane(bit) for bit in range(9)]


def fetch(words, i):
    value = 0
    for bit, word in enumerate(words):
        value = value + (lax.shift_right_logical(word, i) & 1) * (1 << bit)
    return value


def kernel(q_hbm, k_ref, v_ref, id_ref, o_ref,
           q_ref, wide, snd, kv, qst, qaug, feat, ones, top, acc, obuf,
           zsend, zrecv, lsem, qsend, qrecv, osend, orecv, ssem, rsem, qtr):
    s = lax.axis_index("seq")
    g = lax.axis_index("head")
    x, y, zh, c = s // 16, (s // 4) % 4, (s // 2) % 2, s % 2
    col = s // 4
    low = s % 4

    def at(xx, yy):
        return ((xx * 4 + yy) * 4 + low, g)

    def inside(dz, dc, dg):
        return (col * 4 + ((zh + dz) % 2) * 2 + (c + dc) % 2, (g + dg) % 4)

    sibling = inside(0, 1, 0)
    east = at((x + 1) % 4, y)
    plus = at(x, (y + 1) % 4)
    minus = at(x, (y + 3) % 4)
    others = [(dz, dc, dg) for dz in (0, 1) for dc in (0, 1) for dg in (2, 1, 3, 0) if dz or dc or dg]

    load = pltpu.make_async_copy(q_hbm, q_ref, lsem.at[2])
    load.start()

    barrier = pltpu.get_barrier_semaphore()
    peers = [inside(*o) for o in others] + [east, at((x + 3) % 4, y), plus, minus]
    for peer in peers:
        pl.semaphore_signal(barrier, inc=1, device_id=peer, device_id_type=MESH)

    for which, ref in enumerate((k_ref, v_ref)):
        wide[...] = ref[...].astype(jnp.float32)
        for h in range(8):
            snd[h, which * PIECE:(which + 1) * PIECE, :] = wide[pl.ds(h, PIECE, stride=8), :].astype(jnp.bfloat16)

    ids = id_ref[...].astype(jnp.float32)
    first = ids[:, :D]
    second = jnp.concatenate([ids[:, D:], jnp.zeros((1, 2 * D - ROWS), jnp.float32)], axis=1)
    tile = jnp.concatenate([first, second, jnp.zeros((14, D), jnp.float32)], axis=0)
    block = 2 * zh + c
    kv[col, block, HALF:, :] = tile.astype(jnp.bfloat16)

    turned = jnp.transpose(tile[:8])
    lanes = lax.broadcasted_iota(jnp.int32, (D, D), 1).astype(jnp.float32)
    def queries():
        for part, size in ((0, D), (1, ROWS - D)):
            hot = jnp.where(turned[:size, part:part + 1] == lanes[:size], 1.0, 0.0)
            hot = jnp.broadcast_to(hot[:, None, :], (size, GROUP, D)).reshape(size * GROUP, D)
            for which in range(2):
                qst[which, pl.ds(part * D * GROUP, size * GROUP), D:] = hot.astype(jnp.bfloat16)

        def split(t, carry):
            rows = q_ref[pl.ds(t * 16 * 16, 256), :].astype(jnp.float32).reshape(16, 16, D)
            for which in range(2):
                qst[which, pl.ds(t * 128, 128), :D] = (
                    rows[:, 8 * which:8 * which + 8, :].reshape(128, D).astype(jnp.bfloat16))
            return carry

        load.wait()
        lax.fori_loop(0, ROWS // 16, split, 0)

    @pl.when(zh == 0)
    def _():
        queries()

    pl.semaphore_wait(barrier, len(peers))

    spot = pl.ds(pl.multiple_of(2 * PIECE * g, 16), 2 * PIECE)

    def spread(plane):
        for o in others:
            dz, dc, dg = o
            if dz != plane:
                continue
            head = 2 * ((g + dg) % 4) + (c + dc) % 2
            pltpu.make_async_remote_copy(
                src_ref=snd.at[head], dst_ref=kv.at[col, block, spot],
                send_sem=zsend.at[dz], recv_sem=zrecv.at[block],
                device_id=inside(*o), device_id_type=MESH).start()
            if dg == 0:
                pltpu.make_async_remote_copy(
                    src_ref=kv.at[col, block, pl.ds(HALF, 16)], dst_ref=kv.at[col, block, pl.ds(HALF, 16)],
                    send_sem=zsend.at[dz], recv_sem=zrecv.at[block],
                    device_id=inside(*o), device_id_type=MESH).start()

    @pl.when(zh == 0)
    def _():
        spread(0)

    @pl.when(zh == 1)
    def _():
        spread(1)

    pltpu.make_async_copy(snd.at[2 * g + c], kv.at[col, block, spot], lsem.at[0]).start()

    def wait_rows(sem, n):
        pltpu.make_async_copy(feat.at[pl.ds(0, n)], feat.at[pl.ds(0, n)], sem).wait()

    @pl.when(zh == 1)
    def _():
        queries()
        spread(0)

    base = pl.multiple_of(c * MC, MC)
    qcopy = pltpu.make_async_remote_copy(
        src_ref=qst.at[1 - c], dst_ref=qaug.at[pl.ds(base, MC)],
        send_sem=qsend, recv_sem=qrecv, device_id=sibling, device_id_type=MESH)
    qcopy.start()
    qlocal = pltpu.make_async_copy(qst.at[c], qaug.at[pl.ds(base, MC)], lsem.at[1])
    qlocal.start()
    ones[...] = jnp.ones_like(ones)

    @pl.when(zh == 0)
    def _():
        wait_rows(zsend.at[0], 14 * PIECE + 16)
        spread(1)


    def order(t):
        return 2 * ((zh + t // 2) % 2) + (c + t) % 2

    def hands(step, who, b, gox, gop, gom):
        for direction, (go, target) in enumerate(((gox, east), (gop, plus), (gom, minus))):
            @pl.when(go)
            def _(direction=direction, target=target):
                pltpu.make_async_remote_copy(
                    src_ref=kv.at[who, b], dst_ref=kv.at[who, b],
                    send_sem=ssem.at[step, direction], recv_sem=rsem.at[who, b],
                    device_id=target, device_id_type=MESH).start()

    def handed(step, who, gox, gop, gom):
        for direction, go in enumerate((gox, gop, gom)):
            @pl.when(go)
            def _(direction=direction):
                pltpu.make_async_copy(kv.at[who], kv.at[who], ssem.at[step, direction]).wait()

    own = (x < 3, y < 3, y == 0)

    def quarter(who, target, number):
        return pltpu.make_async_remote_copy(
            src_ref=kv.at[who, 3], dst_ref=kv.at[who, 3],
            send_sem=qtr.at[number], recv_sem=rsem.at[who, 3],
            device_id=target, device_id_type=MESH)

    def block_wait(sem):
        pltpu.make_async_copy(kv.at[0, 0], kv.at[0, 0], sem).wait()

    def features(i, who, b, near):
        flip = jnp.transpose(kv[who, b, HALF:, :].astype(jnp.float32)[:8])
        for p, size in ((0, D), (1, ROWS - D)):
            feat[pl.ds(i * ROWS + p * D, size), :] = jnp.where(
                flip[:size, p:p + 1] == lanes[:size], near, -FAR).astype(jnp.bfloat16)

    def scores(r0, keys):
        return lax.dot_general(qaug[pl.ds(r0, SUB), :], keys, (((1,), (1,)), ((), ())),
                               preferred_element_type=jnp.float32)

    def finish(r0, sc, vals, start):
        here = pl.ds(r0, SUB)
        n = sc.shape[1]
        peak = jnp.broadcast_to(jnp.max(sc, axis=1, keepdims=True) * SCALE, (SUB, D))
        if not start:
            old = top[here, :]
            peak = jnp.maximum(old, peak)
        parts = []
        for j in range(0, n, D):
            w = min(D, n - j)
            parts.append(jnp.exp2(sc[:, j:j + w] * SCALE - peak[:, :w]).astype(jnp.bfloat16))
        weights = jnp.concatenate(parts, axis=1)
        out = jnp.dot(weights, vals, preferred_element_type=jnp.float32)
        if start:
            acc[here, :] = out
        else:
            factor = jnp.exp2(old - peak)
            acc[here, :D] = acc[here, :D] * factor + out[:, :D]
            acc[here, D:] = acc[here, D:] * factor + out[:, D:]
        top[here, :] = peak

    def attend(r, blocks, start, unroll):
        n = len(blocks) * ROWS

        def keys():
            k = jnp.concatenate([kv[who, b, r0:r0 + PIECE, :] for who, b in blocks
                                 for r0 in range(0, HALF, 2 * PIECE)], axis=0)
            return jnp.concatenate([k, feat[:n, :]], axis=1)

        def vals():
            v = jnp.concatenate([kv[who, b, r0:r0 + PIECE, :] for who, b in blocks
                                 for r0 in range(PIECE, HALF, 2 * PIECE)], axis=0)
            return jnp.concatenate([v, ones[:n, :]], axis=1)

        sc = scores(r, keys())
        for u in range(unroll):
            here = r + u * SUB
            nxt = scores(here + SUB, keys()) if u + 1 < unroll else None
            if start:
                shape = (SUB, n)
                row = here + lax.broadcasted_iota(jnp.int32, shape, 0)
                when = lax.broadcasted_iota(jnp.int32, shape, 1)
                sc = jnp.where(when * GROUP <= row, sc, -FAR)
            finish(here, sc, vals(), start)
            sc = nxt

    def mark(blocks, nears):
        for i, ((who, b), near) in enumerate(zip(blocks, nears)):
            features(i, who, b, near)

    def sweep(blocks, nears, start, count, unroll):
        mark(blocks, nears)

        def body(t, carry):
            attend(pl.multiple_of(t * (SUB * unroll), SUB * unroll), blocks, start, unroll)
            return carry

        lax.fori_loop(0, count // (SUB * unroll), body, 0)

    wait_rows(lsem.at[0], 2 * PIECE)
    wait_rows(zrecv.at[block], 6 * PIECE)
    hands(0, col, block, *own)
    block_wait(zrecv.at[order(1)])
    hands(0, col, order(1), *own)
    qlocal.wait()
    qcopy.wait_recv()
    sweep([(col, 2 * zh), (col, 2 * zh + 1)], [0.0] * 2, True, M, 4)

    orders = by_lane(PLANES, y)
    back_w, lane_w, gox_w, gop_w, gom_w = by_lane((BACK, LANE, GOX, GOP, GOM), y)

    def step_of(k, t):
        bit = jnp.where(t == 3, 2, 1)
        back = pick(back_w, k)
        who = (x - back) * 4 + pick(lane_w, k)
        there = x >= back
        gox = there & ((pick(gox_w, k) & bit) > 0) & (x < 3)
        gop = there & ((pick(gop_w, k) & bit) > 0)
        gom = there & ((pick(gom_w, k) & bit) > 0)
        lone = (zh == 0) & (x == 2) & (y == 3) & (who == 3)
        return who, there, gox, gop, gom, lone

    def onward(k, t):
        who, there, gox, gop, gom, lone = step_of(k, t)
        b = order(t)

        @pl.when(gox | gop | gom)
        def _():
            block_wait(rsem.at[who, b])
            hands(k + 1, who, b, gox, gop, gom)

            @pl.when(lone & (b == 3))
            def _():
                quarter(who, east, 0).start()

    corner = (zh == 0) & (x == 3)

    def pairs_of(op):
        blocks, nears, present = [], [], []
        for pair in ((op % 256) // 16, op % 16):
            pairs = []
            for j in range(2):
                t = 2 * (pair % 2) + j
                who, there, gox, gop, gom, lone = step_of(pair // 2, t)
                b = order(t)
                pairs.append(b)

                @pl.when(there & jnp.logical_not(gox | gop | gom))
                def _(who=who, b=b):
                    block_wait(rsem.at[who, b])

            blocks += [(jnp.where(there, who, col), b) for b in pairs]
            nears += [jnp.where(there, 0.0, -FAR)] * 2
            present.append(there)
        return blocks, nears, present[0] | present[1]

    def turn(i, carry):
        op = fetch(orders, i)

        @pl.when(op < 32)
        def _():
            onward(op // 4, op % 4)

        @pl.when((op >= 32) & (op < 64))
        def _():
            b = order(op % 4)
            block_wait(zrecv.at[b])
            hands(0, col, b, *own)

        @pl.when((op == 64) & (zh == 1))
        def _():
            sweep([(col, 0), (col, 1)], [0.0] * 2, False, M, 4)

        @pl.when(op >= 256)
        def _():
            blocks, nears, present = pairs_of(op)

            @pl.when(present)
            def _():
                sweep(blocks, nears, False, M, 4)

        @pl.when((i == LATE) & (zh == 0) & (x >= 2) & (y < 3))
        def _():
            quarter(col - 8, plus, 0).start()

        @pl.when((i == RELAY) & corner & (y == 3))
        def _():
            block_wait(rsem.at[3, 3])
            quarter(3, plus, 1).start()

        return carry

    last = len(ORDER[0]) - 1
    lax.fori_loop(0, last, turn, 0)

    @pl.when(((zh == 0) & (x >= 2) & (y >= 1)) | (corner & (y == 0)))
    def _():
        who = col - 9
        block_wait(rsem.at[who, 3])
        sweep([(who, 3)], [0.0], False, MC, 2)

    def result(b, ref, slot):
        def body(t, carry):
            here = pl.ds(pl.multiple_of(b * MC + t * 256, 256), 256)
            ref[slot, pl.ds(t * 256, 256), :] = (acc[here, :D] / acc[here, D:]).astype(jnp.bfloat16)
            return carry

        lax.fori_loop(0, MC // 256, body, 0)

    ocopy = pltpu.make_async_remote_copy(
        src_ref=obuf.at[0], dst_ref=o_ref.at[c],
        send_sem=osend, recv_sem=orecv, device_id=sibling, device_id_type=MESH)
    blocks, nears, present = pairs_of(fetch(orders, last))
    mark(blocks, nears)

    def final(h, carry):
        b = (1 - c + h) % 2

        @pl.when(present)
        def _():
            attend(pl.multiple_of(b * MC, MC), blocks, False, MC // SUB)

        @pl.when(h == 0)
        def _():
            result(b, obuf, 0)
            ocopy.start()

        @pl.when(h == 1)
        def _():
            result(b, o_ref, c)

        return carry

    lax.fori_loop(0, 2, final, 0)
    ocopy.wait_recv()

    ocopy.wait_send()
    qcopy.wait_send()
    @pl.when(zh == 1)
    def _():
        wait_rows(zsend.at[0], 14 * PIECE + 16)

    pltpu.make_async_copy(kv.at[0, pl.ds(0, 2)], kv.at[0, pl.ds(0, 2)], zsend.at[1]).wait()
    handed(0, col, *own)

    for lane in range(4):
        @pl.when(y == lane)
        def _(lane=lane):
            for k, (back, _, gox, gop, gom) in enumerate(PLAN[lane]):
                if gox or gop or gom:
                    @pl.when(x >= back)
                    def _(k=k, go=(gox, gop, gom)):
                        for direction in range(3):
                            if go[direction]:
                                @pl.when((x < 3) | (direction > 0))
                                def _(direction=direction):
                                    some = kv.at[0, pl.ds(0, (0, 3, 1, 4)[go[direction]])]
                                    pltpu.make_async_copy(some, some, ssem.at[k + 1, direction]).wait()

    @pl.when((zh == 0) & ((x == 2) | ((x == 3) & (y < 3))))
    def _():
        block_wait(qtr.at[0])

    @pl.when(corner & (y == 3))
    def _():
        block_wait(qtr.at[1])


def per_device(queries, keys, values, doc_ids):
    bf, f32 = jnp.bfloat16, jnp.float32
    dma = pltpu.SemaphoreType.DMA
    vmem = pl.BlockSpec(memory_space=pltpu.VMEM)
    out = pl.pallas_call(
        kernel,
        out_shape=jax.ShapeDtypeStruct((2, MC, D), bf),
        in_specs=[pl.BlockSpec(memory_space=pl.ANY)] + [vmem] * 3,
        out_specs=vmem,
        scratch_shapes=[
            pltpu.VMEM((ROWS * 16, D), bf),
            pltpu.VMEM((8 * PIECE, D), f32),
            pltpu.VMEM((8, 2 * PIECE, D), bf),
            pltpu.VMEM((16, 4, CHUNK, D), bf),
            pltpu.VMEM((2, MC, 2 * D), bf),
            pltpu.VMEM((M, 2 * D), bf),
            pltpu.VMEM((KEYS, D), bf),
            pltpu.VMEM((KEYS, D), bf),
            pltpu.VMEM((M, D), f32),
            pltpu.VMEM((M, 2 * D), f32),
            pltpu.VMEM((1, MC, D), bf),
            dma((2,)), dma((4,)), dma((3,)), dma, dma, dma, dma,
            dma((STEPS + 1, 3)), dma((16, 4)), dma((2,)),
        ],
        compiler_params=pltpu.CompilerParams(
            collective_id=0, has_side_effects=True, vmem_limit_bytes=56 * 1024 * 1024),
    )(queries.reshape(ROWS * 16, D), keys.reshape(8 * PIECE, D), values.reshape(8 * PIECE, D),
      doc_ids.reshape(1, ROWS))
    return jnp.swapaxes(out.reshape(2, ROWS, GROUP, D), 0, 1).reshape(ROWS, 2 * GROUP, D)


def solution(mesh):
    return jax.shard_map(
        per_device,
        mesh=mesh,
        in_specs=(
            P("seq", "head", None),
            P(("seq", "head"), None, None),
            P(("seq", "head"), None, None),
            P("seq"),
        ),
        out_specs=P("seq", "head", None),
        check_vma=False,
    )
```
